256 devices in a mesh: leaf: 64 (over x, z, core), probe: 4 (over y).
Axes of the slice: x: 4, y: 4, z: 8, core: 2. Of those that a mesh axis runs over, the one named last changes fastest.
Arguments:
- probes: float32 [64, 131072], P('probe', 'leaf'), parts along dimension 0, may hold values from -6 to 6
- perm: int32 [131072], P('leaf'), may hold values from 0 to 131071, as said below
- points: float32 [3, 131072], P(None, 'leaf'), may hold values from -4.2 to 4.2
- anchors: float32 [3, 32768], P(None, 'leaf'), may hold values from -4.2 to 4.2
- trans_low: bfloat16 [64, 6, 128, 128], P('leaf'), may hold values from -0.375 to 0.375
- couple_low: bfloat16 [64, 3, 128, 128], P('leaf'), may hold values from -0.25 to 0.25
- trans_top: bfloat16 [126, 128, 128], replicated, may hold values from -0.375 to 0.375
- couple_top: bfloat16 [63, 128, 128], replicated, may hold values from -0.25 to 0.25
Outputs:
- kernel_times: float32 [64, 131072], P('probe', 'leaf'), parts along dimension 0
The draws below stay inside these ranges and needn't reach their ends.
There are 4 independent parts, one for each index of `probe`. The reference program is written for one: setup_inputs(seed, part) draws one part's arguments, and reference() takes and returns one part's arrays. A program takes and returns all parts, laid end to end along the dimension named above; an argument that names none is the same for every part. Nothing has to cross between parts.
Inputs may be any that keep to these rules, and one draw needn't show every extreme that they name: perm is a permutation of the 131072 points; the 2048 positions of each device take exactly 32 points from the 2048 initial points of every device.
All inputs are finite; a program needn't handle non-finite values.
Results may differ from the reference program's by a relative error of at most 0.0003.
Values sent between devices are 32-bit elements; how exact they have to be, the bound alone decides.
A program may use at most 64 MiB of HBM per device.

```python
import jax
import jax.numpy as jnp
from jax import lax

LEAF = 512
R = 128
PRB = 16
DIMS = 3
L_DEV = 4
PTS_DEV = 2048
LEAVES = 256
NPTS = 131072
N_LEAF = 64


def draw_perm(key, part):
    key = jax.random.fold_in(key, 11)
    source_key, target_key = jax.random.split(key)
    block_len = PTS_DEV // N_LEAF

    def shuffled(row_key):
        return jax.random.permutation(row_key, PTS_DEV).astype(jnp.int32)
    within = jax.vmap(shuffled)(jax.random.split(source_key, N_LEAF))
    home_index = within + (jnp.arange(N_LEAF, dtype=jnp.int32) * PTS_DEV)[:, None]
    routed = home_index.reshape(N_LEAF, N_LEAF, block_len).transpose(1, 0, 2).reshape(N_LEAF, PTS_DEV)

    def mixed_row(row_key, row_vals):
        return jax.random.permutation(row_key, row_vals)
    mixed = jax.vmap(mixed_row)(jax.random.split(target_key, N_LEAF), routed)
    return mixed.reshape(-1).astype(jnp.int32)


def block_levels(rng, extent, shards, low, top_value):
    factor_of, own = 1.0, jax.random.fold_in(rng, 6)
    for dim, blocks in shards:
        draws = jnp.exp(jax.random.uniform(jax.random.fold_in(own, dim), (blocks,), jnp.float32, low / len(shards), top_value / len(shards)))
        factor_of = factor_of * jnp.repeat(draws, extent[dim] // blocks).reshape([-1 if axis == dim else 1 for axis in range(len(extent))])
    return factor_of


def normal_values(own_key, dims, width, most, cuts=(), kind=jnp.bfloat16):
    gain = block_levels(own_key, dims, cuts, -0.22, 0.18) if cuts else 1.0
    drawn = jax.random.normal(own_key, dims, jnp.float32) * width * gain
    return jnp.minimum(jnp.maximum(drawn, -most), most).astype(kind)


def setup_inputs(seed: int = 0, part: int = 0) -> dict:
    arg_keys = jax.random.split(jax.random.key(seed), 9)
    part_keys = jax.random.split(jax.random.fold_in(arg_keys[8], part), 9)
    return {
        "probes": normal_values(part_keys[0], (PRB, NPTS), 1.0, 6.0, ((1, 64),), jnp.float32),
        "perm": draw_perm(jax.random.fold_in(arg_keys[8], 71), part),
        "points": normal_values(arg_keys[2], (DIMS, NPTS), 0.7, 4.2, ((1, 64),), jnp.float32),
        "anchors": normal_values(arg_keys[3], (DIMS, LEAVES * R), 0.7, 4.2, ((1, 64),), jnp.float32),
        "trans_low": normal_values(arg_keys[4], (N_LEAF, 2 * L_DEV - 2, R, R), (2 * R) ** -0.5, 0.375, ((0, 64),)),
        "couple_low": normal_values(arg_keys[5], (N_LEAF, L_DEV - 1, R, R), (4 * R) ** -0.5, 0.25, ((0, 64),)),
        "trans_top": normal_values(arg_keys[6], (2 * N_LEAF - 2, R, R), (2 * R) ** -0.5, 0.375),
        "couple_top": normal_values(arg_keys[7], (N_LEAF - 1, R, R), (4 * R) ** -0.5, 0.25),
    }


EXACT_MATMUL = lax.Precision.HIGHEST
SHARPNESS = 2.0
OUTPUT_SCALE = 0.25
NOISE_VAR = 0.5


def kernel_block(left_pts, right_pts):
    distance = jnp.zeros((left_pts.shape[1], right_pts.shape[1]), jnp.float32)
    for coord in range(left_pts.shape[0]):
        differ = left_pts[coord][:, None] - right_pts[coord][None, :]
        distance = distance + differ * differ
    return jnp.exp(-SHARPNESS * distance)


def level_transfer(trans_low, trans_top, height, local_levels):
    if height < local_levels:
        node_total = L_DEV >> height
        node_start = sum(L_DEV >> lower for lower in range(height))
        picked = trans_low[:, node_start:node_start + node_total]
        return picked.reshape(N_LEAF * node_total, R, R).astype(jnp.float32)
    upper = height - local_levels
    node_total = N_LEAF >> upper
    node_start = sum(N_LEAF >> lower for lower in range(upper))
    return trans_top[node_start:node_start + node_total].astype(jnp.float32)


def level_coupling(couple_low, couple_top, height, local_levels):
    if height < local_levels:
        pair_count = L_DEV >> (height + 1)
        pair_start = sum(L_DEV >> (lower + 1) for lower in range(height))
        picked = couple_low[:, pair_start:pair_start + pair_count]
        return picked.reshape(N_LEAF * pair_count, R, R).astype(jnp.float32)
    upper = height - local_levels
    pair_count = N_LEAF >> (upper + 1)
    pair_start = sum(N_LEAF >> (lower + 1) for lower in range(upper))
    return couple_top[pair_start:pair_start + pair_count].astype(jnp.float32)


def reference(probes, perm, points, anchors, trans_low, couple_low, trans_top, couple_top):
    local_levels = L_DEV.bit_length() - 1
    levels = local_levels + N_LEAF.bit_length() - 1
    leaf_total = L_DEV * N_LEAF
    reordered = probes[:, perm]
    leaf_probes = reordered.reshape(PRB, leaf_total, LEAF).transpose(1, 0, 2)
    leaf_points = points.reshape(points.shape[0], leaf_total, LEAF).transpose(1, 0, 2)
    leaf_anchors = anchors.reshape(anchors.shape[0], leaf_total, R).transpose(1, 0, 2)

    def upward_leaf(pieces):
        values, spots, centres = pieces
        near_field = jnp.dot(values, kernel_block(spots, spots), precision=EXACT_MATMUL)
        expansion_weights = jnp.dot(values, kernel_block(spots, centres), precision=EXACT_MATMUL)
        return near_field, expansion_weights

    near_field, bottom = lax.map(upward_leaf, (leaf_probes, leaf_points, leaf_anchors))
    ascent = [bottom]
    for height in range(levels - 1):
        transfer = level_transfer(trans_low, trans_top, height, local_levels)
        moved = jnp.einsum("npr,nrs->nps", ascent[-1], transfer, precision=EXACT_MATMUL)
        ascent.append(moved.reshape(-1, 2, PRB, R).sum(axis=1))
    downward_sweep = None
    for height in range(levels - 1, -1, -1):
        current = ascent[height]
        coupling = level_coupling(couple_low, couple_top, height, local_levels)
        to_left = jnp.einsum("npr,nrs->nps", current[1::2], coupling, precision=EXACT_MATMUL)
        to_right = jnp.einsum("npr,nsr->nps", current[0::2], coupling, precision=EXACT_MATMUL)
        coupled = jnp.stack([to_left, to_right], axis=1).reshape(current.shape)
        if downward_sweep is None:
            downward_sweep = coupled
        else:
            transfer = level_transfer(trans_low, trans_top, height, local_levels)
            parents = jnp.repeat(downward_sweep, 2, axis=0)
            downward_sweep = coupled + jnp.einsum("npr,nsr->nps", parents, transfer, precision=EXACT_MATMUL)

    def downward_leaf(pieces):
        values, spots, centres, near_part, incoming = pieces
        distant_interaction = jnp.dot(incoming, kernel_block(spots, centres).T, precision=EXACT_MATMUL)
        return OUTPUT_SCALE * (near_part + distant_interaction) + NOISE_VAR * values

    result = lax.map(downward_leaf, (leaf_probes, leaf_points, leaf_anchors, near_field, downward_sweep))
    result = result.transpose(1, 0, 2).reshape(PRB, leaf_total * LEAF)
    return jnp.zeros_like(result).at[:, perm].set(result)
```

```python
import functools

import jax
import jax.numpy as jnp
from jax import lax
from jax.experimental import pallas as pl
from jax.experimental.pallas import tpu as pltpu
from jax.sharding import PartitionSpec as P

LEAF = 512
R = 128
PRB = 16
L_DEV = 4
PTS = 2048
N = 64
BLK = PTS // N
TILES = PTS // 128
SHARPNESS = 2.0
OUTPUT_SCALE = 0.25
NOISE_VAR = 0.5
MESH = pl.DeviceIdType.MESH
F32 = jnp.float32
BF16 = jnp.bfloat16
I32 = jnp.int32


def dot(a, b):
    return jnp.dot(a, b, preferred_element_type=F32)


def dot_nt(a, b):
    return lax.dot_general(a, b, (((1,), (1,)), ((), ())), preferred_element_type=F32)


def split(v):
    hi = v.astype(BF16)
    lo = (v - hi.astype(F32)).astype(BF16)
    return hi, lo


def pair(v):
    hi, lo = split(v)
    return jnp.concatenate([hi, lo], axis=0)


def fold(r):
    return r[:PRB] + r[PRB:]


def iota(shape, dim):
    return lax.broadcasted_iota(I32, shape, dim)


def swap_blocks(tile):
    lane = iota((8, 128), 1)
    row = iota((8, 128), 0)
    v0, v1 = tile[:8], tile[8:]
    low = lane < 64
    a0 = jnp.where(low, v0, pltpu.roll(v1, 64, 1))
    a1 = jnp.where(low, pltpu.roll(v0, 64, 1), v1)
    lane_bit = (lane >> 5) & 1
    same = (row >> 2) == lane_bit
    outs = []
    for a in (a0, a1):
        y = pltpu.roll(a, 4, 0)
        moved = jnp.where(lane_bit == 1, pltpu.roll(y, 32, 1), pltpu.roll(y, 96, 1))
        outs.append(jnp.where(same, a, moved))
    return outs


def gather_tile(source, index_row):
    index = jnp.broadcast_to(index_row, (8, 128))
    lane = index & 127
    tile = index >> 7
    out0 = jnp.zeros((8, 128), F32)
    out1 = jnp.zeros((8, 128), F32)
    for s in range(TILES):
        v = source(s)
        here = tile == s
        g0 = jnp.take_along_axis(v[:8], lane, axis=1, mode="promise_in_bounds")
        g1 = jnp.take_along_axis(v[8:], lane, axis=1, mode="promise_in_bounds")
        out0 = jnp.where(here, g0, out0)
        out1 = jnp.where(here, g1, out1)
    return jnp.concatenate([out0, out1], axis=0)


def by_lane_block(rows):
    block = iota((1, 128), 1) >> 5
    out = rows[3]
    for b in (2, 1, 0):
        out = jnp.where(block == b, rows[b], out)
    return out


def kernel(
    perm_h, points_h, anchors_h, probes_h, tl_h, cl_h, tt_h, ct_h,
    out_v,
    perm_v, points_v, anchors_v, probes_v, tl_v, cl_v,
    e0_v, e1_v, e2_v, e3_v, e4_v, ct_v, cs_v,
    slot_v, inv_v, asked_v, back_v,
    ptst_v, dhi_v, dlo_v, bhi_v, blo_v,
    x_v, x2_v, xs_v, y_v, near_v,
    idx_s, idx_r, a_s, a_r, b_s, b_r,
    q0_v, q1_v, q2_v, q3_v, q4_v, q5_v,
    load_sem, send_sem, recv_sem, own_sem,
):
    me = lax.axis_index("leaf")
    group = me // 8
    pos = me % 8

    loads = [
        pltpu.make_async_copy(perm_h, perm_v, load_sem.at[0]),
        pltpu.make_async_copy(points_h, points_v.at[pl.ds(0, 3)], load_sem.at[1]),
        pltpu.make_async_copy(anchors_h, anchors_v, load_sem.at[2]),
        pltpu.make_async_copy(probes_h, probes_v, load_sem.at[3]),
        pltpu.make_async_copy(tl_h.at[0], tl_v, load_sem.at[4]),
        pltpu.make_async_copy(cl_h.at[0], cl_v, load_sem.at[5]),
        pltpu.make_async_copy(tt_h.at[pl.ds(group * 8, 8)], e0_v, load_sem.at[6]),
        pltpu.make_async_copy(tt_h.at[pl.ds(64 + group * 4, 4)], e1_v, load_sem.at[7]),
        pltpu.make_async_copy(tt_h.at[pl.ds(96 + group * 2, 2)], e2_v, load_sem.at[8]),
        pltpu.make_async_copy(tt_h.at[pl.ds(112, 8)], e3_v, load_sem.at[9]),
        pltpu.make_async_copy(tt_h.at[pl.ds(120, 4)], e4_v, load_sem.at[10]),
    ]
    for t, start in enumerate((0, 32, 48, 56, 60, 62)):
        loads.append(
            pltpu.make_async_copy(
                ct_h.at[pl.ds(start + me // (2 << t), 1)], ct_v.at[pl.ds(t, 1)], load_sem.at[11 + t]
            )
        )
    for copy in loads:
        copy.start()

    barrier = pltpu.get_barrier_semaphore()

    @pl.loop(1, N)
    def _(k):
        pl.semaphore_signal(barrier, inc=1, device_id={"leaf": (me + k) % N}, device_id_type=MESH)

    def remote(src, dst, which, peer):
        return pltpu.make_async_remote_copy(
            src_ref=src, dst_ref=dst, send_sem=send_sem.at[which], recv_sem=recv_sem.at[which],
            device_id={"leaf": peer}, device_id_type=MESH,
        )

    loads[0].wait()
    row64 = iota((N, 128), 0)
    lane1 = iota((1, 128), 1)
    ones = []
    for b in range(TILES):
        home = perm_v[b : b + 1, :] >> 11
        ones.append((row64 == home).astype(F32))
    before = (iota((128, 128), 0) < iota((128, 128), 1)).astype(BF16)
    counter = jnp.concatenate([before, jnp.ones((128, 128), BF16)], axis=1)
    counts = dot(jnp.concatenate(ones, axis=0).astype(BF16), counter)
    base = jnp.zeros((N, 128), F32)
    found = jnp.zeros((4 * N, 128), F32)
    row128 = iota((128, 128), 0) & (BLK - 1)
    for b in range(TILES):
        entry = perm_v[b : b + 1, :]
        one = ones[b]
        rank = jnp.sum(one * (counts[N * b : N * (b + 1), :128] + base), axis=0, keepdims=True)
        base = base + counts[N * b : N * (b + 1), 128:]
        rank = rank.astype(I32)
        slot_v[b : b + 1, :] = (entry >> 11) * BLK + rank
        offset = entry & (PTS - 1)
        left = jnp.concatenate(
            [
                one * (offset >> 8).astype(F32),
                one * (offset & 255).astype(F32),
                one * float(b),
                one * lane1.astype(F32),
            ],
            axis=0,
        ).astype(BF16)
        right = (row128 == rank).astype(F32).astype(BF16)
        found = found + dot_nt(left, right)
    wanted = (found[:N] * 256.0 + found[N : 2 * N]).astype(I32)
    places = (found[2 * N : 3 * N] * 128.0 + found[3 * N :]).astype(I32)
    for h in range(N):
        idx_s[h] = wanted[h : h + 1, :]
    for o in range(TILES):
        inv_v[o : o + 1, :] = by_lane_block([places[4 * o + b : 4 * o + b + 1, :] for b in range(4)])

    pl.semaphore_wait(barrier, N - 1)

    @pl.loop(1, N)
    def _(k):
        peer = (me + k) % N
        remote(idx_s.at[peer], idx_r.at[me], 0, peer).start()

    own = pltpu.make_async_copy(idx_s.at[me], idx_r.at[me], own_sem.at[0])
    own.start()

    loads[1].wait()
    loads[2].wait()
    for b in range(TILES):
        ptst_v[128 * b : 128 * (b + 1), :] = jnp.transpose(points_v[:, 128 * b : 128 * (b + 1)])

    rows = 64

    @pl.loop(0, PTS // rows)
    def _(i):
        at = pl.ds(pl.multiple_of(i * rows, rows), rows)
        leaf = i // (LEAF // rows)
        total = None
        for c in range(3):
            left = ptst_v[at, c : c + 1]
            right = anchors_v[c : c + 1, pl.ds(pl.multiple_of(leaf * R, R), R)]
            differ = left - right
            total = differ * differ if total is None else total + differ * differ
        hi, lo = split(jnp.exp(-SHARPNESS * total))
        bhi_v[at, :] = hi
        blo_v[at, :] = lo

    own.wait()
    remote(idx_s.at[pl.ds(0, N - 1)], idx_r.at[pl.ds(0, N - 1)], 0, me).wait()

    for o in range(TILES):
        asked_v[o : o + 1, :] = by_lane_block([idx_r[4 * o + b] for b in range(4)])

    loads[3].wait()

    def send_tile(tile, o, s_ref, r_ref, which, own_at):
        halves = swap_blocks(tile)
        for h in range(4):
            s_ref[4 * o + h] = halves[h // 2][4 * (h % 2) : 4 * (h % 2) + 4]
        for h in range(4):
            peer = 4 * o + h

            @pl.when(peer != me)
            def _():
                remote(s_ref.at[peer], r_ref.at[me], which, peer).start()

            @pl.when(peer == me)
            def _():
                pltpu.make_async_copy(s_ref.at[peer], r_ref.at[me], own_sem.at[own_at]).start()

    def receive_tiles(s_ref, r_ref, which, own_at):
        pltpu.make_async_copy(s_ref.at[me], r_ref.at[me], own_sem.at[own_at]).wait()
        remote(s_ref.at[pl.ds(0, N - 1)], r_ref.at[pl.ds(0, N - 1)], which, me).wait()

        @pl.loop(0, TILES)
        def _(o):
            parts = [r_ref[4 * o + h] for h in range(4)]
            both = jnp.concatenate(parts, axis=0)
            out = swap_blocks(both)
            xs_v[o] = jnp.concatenate(out, axis=0)

    @pl.loop(0, TILES)
    def _(i):
        o = (me // 4 + i) % TILES
        tile = gather_tile(lambda s: probes_v[:, 128 * s : 128 * (s + 1)], asked_v[pl.ds(o, 1), :])
        send_tile(tile, o, a_s, a_r, 1, 1)

    drows = 32

    @pl.loop(0, PTS // drows)
    def _(i):
        at = pl.ds(pl.multiple_of(i * drows, drows), drows)
        leaf = i // (LEAF // drows)
        total = None
        for c in range(3):
            left = ptst_v[at, c : c + 1]
            right = points_v[c : c + 1, pl.ds(pl.multiple_of(leaf * LEAF, LEAF), LEAF)]
            differ = left - right
            total = differ * differ if total is None else total + differ * differ
        hi, lo = split(jnp.exp(-SHARPNESS * total))
        dhi_v[at, :] = hi
        dlo_v[at, :] = lo

    found = jnp.zeros((2 * TILES, 128), F32)
    row16 = iota((TILES, 128), 0)
    row128 = iota((128, 128), 0)
    for o in range(TILES):
        asked = asked_v[o : o + 1, :]
        one = (row16 == (asked >> 7)).astype(F32)
        left = jnp.concatenate([one * float(o), one * lane1.astype(F32)], axis=0).astype(BF16)
        right = (row128 == (asked & 127)).astype(F32).astype(BF16)
        found = found + dot_nt(left, right)
    back_v[...] = (found[:TILES] * 128.0 + found[TILES:]).astype(I32)

    for copy in loads[4:]:
        copy.wait()
    for t in range(6):
        mat = ct_v[t].astype(F32)
        odd = (me // (1 << t)) % 2
        cs_v[t] = jnp.where(odd == 1, jnp.transpose(mat), mat).astype(BF16)

    receive_tiles(a_s, a_r, 1, 1)

    @pl.loop(0, TILES)
    def _(o):
        tile = gather_tile(lambda s: xs_v[s], slot_v[pl.ds(o, 1), :])
        at = pl.ds(pl.multiple_of(o * 128, 128), 128)
        x_v[:, at] = tile
        x2_v[:, at] = pair(tile)

    def up(children, transfers):
        lhs = pair(jnp.concatenate(children, axis=1))
        return fold(dot(lhs, transfers.reshape(2 * R, R)))

    leaves = []
    for i in range(L_DEV):
        x2 = x2_v[:, LEAF * i : LEAF * (i + 1)]
        at = slice(LEAF * i, LEAF * (i + 1))
        leaves.append(fold(dot(x2, bhi_v[at, :])) + dot(x2[:PRB], blo_v[at, :]))
    mids = [up(leaves[2 * n : 2 * n + 2], tl_v[2 * n : 2 * n + 2]) for n in range(2)]
    q0_v[pos] = up(mids, tl_v[4:6])

    @pl.loop(1, 8)
    def _(k):
        peer = group * 8 + (pos + k) % 8
        remote(q0_v.at[pos], q0_v.at[pos], 2, peer).start()

    def near(i):
        x2 = x2_v[:, LEAF * i : LEAF * (i + 1)]
        at = slice(LEAF * i, LEAF * (i + 1))
        near_v[:, at] = fold(dot(x2, dhi_v[at, :])) + dot(x2[:PRB], dlo_v[at, :])

    near(0)
    near(1)
    remote(q0_v.at[pl.ds(0, 7)], q0_v.at[pl.ds(0, 7)], 2, me).wait()
    for n in range(4):
        q1_v[n] = up([q0_v[2 * n], q0_v[2 * n + 1]], e0_v[2 * n : 2 * n + 2])
    for n in range(2):
        q2_v[n] = up([q1_v[2 * n], q1_v[2 * n + 1]], e1_v[2 * n : 2 * n + 2])
    q3_v[group] = up([q2_v[0], q2_v[1]], e2_v[...])

    @pl.loop(1, 8)
    def _(k):
        peer = ((group + k) % 8) * 8 + pos
        remote(q3_v.at[group], q3_v.at[group], 3, peer).start()

    near(2)
    near(3)
    remote(q3_v.at[pl.ds(0, 7)], q3_v.at[pl.ds(0, 7)], 3, me).wait()
    for n in range(4):
        q4_v[n] = up([q3_v[2 * n], q3_v[2 * n + 1]], e3_v[2 * n : 2 * n + 2])
    for n in range(2):
        q5_v[n] = up([q4_v[2 * n], q4_v[2 * n + 1]], e4_v[2 * n : 2 * n + 2])

    def other(index):
        return index + 1 - 2 * (index % 2)

    def coupled(q, matrix):
        return fold(dot(pair(q), matrix))

    def down(g, matrix):
        return fold(dot_nt(pair(g), matrix))

    g = coupled(q5_v[other(group // 4)], cs_v[5])
    g = coupled(q4_v[other(group // 2)], cs_v[4]) + down(g, e4_v[group // 2])
    g = coupled(q3_v[other(group)], cs_v[3]) + down(g, e3_v[group])
    g = coupled(q2_v[other(pos // 4)], cs_v[2]) + down(g, e2_v[pos // 4])
    g = coupled(q1_v[other(pos // 2)], cs_v[1]) + down(g, e1_v[pos // 2])
    g = coupled(q0_v[other(pos)], cs_v[0]) + down(g, e0_v[pos])

    def both_down(q_even, q_odd, coupling, g, e_even, e_odd):
        even = fold(dot(pair(q_odd), coupling)) + down(g, e_even)
        odd = fold(dot_nt(pair(q_even), coupling)) + down(g, e_odd)
        return even, odd

    g_mids = both_down(mids[0], mids[1], cl_v[2], g, tl_v[4], tl_v[5])
    for n in range(2):
        g_leaves = both_down(
            leaves[2 * n], leaves[2 * n + 1], cl_v[n], g_mids[n], tl_v[2 * n], tl_v[2 * n + 1]
        )
        for s in range(2):
            i = 2 * n + s
            at = slice(LEAF * i, LEAF * (i + 1))
            hi, lo = split(g_leaves[s])
            both = jnp.concatenate([hi, lo], axis=0)
            far = fold(dot_nt(both, bhi_v[at, :])) + dot_nt(hi, blo_v[at, :])
            y = OUTPUT_SCALE * (near_v[:, at] + far) + NOISE_VAR * x_v[:, at]
            for b in range(4):
                y_v[4 * i + b] = y[:, 128 * b : 128 * (b + 1)]

    @pl.loop(0, TILES)
    def _(i):
        o = (me // 4 + i) % TILES
        tile = gather_tile(lambda s: y_v[s], inv_v[pl.ds(o, 1), :])
        send_tile(tile, o, b_s, b_r, 4, 2)

    receive_tiles(b_s, b_r, 4, 2)

    @pl.loop(0, TILES)
    def _(o):
        at = pl.ds(pl.multiple_of(o * 128, 128), 128)
        out_v[:, at] = gather_tile(lambda s: xs_v[s], back_v[pl.ds(o, 1), :])


def body(probes, perm, points, anchors, trans_low, couple_low, trans_top, couple_top):
    vmem = pltpu.VMEM
    dma = pltpu.SemaphoreType.DMA
    return pl.pallas_call(
        kernel,
        out_shape=jax.ShapeDtypeStruct((PRB, PTS), F32),
        in_specs=[pl.BlockSpec(memory_space=pl.ANY)] * 8,
        out_specs=pl.BlockSpec(memory_space=pltpu.VMEM),
        scratch_shapes=[
            vmem((TILES, 128), I32),
            vmem((8, PTS), F32),
            vmem((3, L_DEV * R), F32),
            vmem((PRB, PTS), F32),
            vmem((6, R, R), BF16),
            vmem((3, R, R), BF16),
            vmem((8, R, R), BF16),
            vmem((4, R, R), BF16),
            vmem((2, R, R), BF16),
            vmem((8, R, R), BF16),
            vmem((4, R, R), BF16),
            vmem((6, R, R), BF16),
            vmem((6, R, R), BF16),
            vmem((TILES, 128), I32),
            vmem((TILES, 128), I32),
            vmem((TILES, 128), I32),
            vmem((TILES, 128), I32),
            vmem((PTS, 8), F32),
            vmem((PTS, LEAF), BF16),
            vmem((PTS, LEAF), BF16),
            vmem((PTS, R), BF16),
            vmem((PTS, R), BF16),
            vmem((PRB, PTS), F32),
            vmem((2 * PRB, PTS), BF16),
            vmem((TILES, PRB, 128), F32),
            vmem((TILES, PRB, 128), F32),
            vmem((PRB, PTS), F32),
            vmem((N, 1, 128), I32),
            vmem((N, 1, 128), I32),
            vmem((N, 4, 128), F32),
            vmem((N, 4, 128), F32),
            vmem((N, 4, 128), F32),
            vmem((N, 4, 128), F32),
            vmem((8, PRB, R), F32),
            vmem((4, PRB, R), F32),
            vmem((2, PRB, R), F32),
            vmem((8, PRB, R), F32),
            vmem((4, PRB, R), F32),
            vmem((2, PRB, R), F32),
            dma((17,)),
            dma((5,)),
            dma((5,)),
            dma((3,)),
        ],
        compiler_params=pltpu.CompilerParams(
            collective_id=0, has_side_effects=True, vmem_limit_bytes=40 * 1024 * 1024
        ),
        name="hss_product",
    )(perm.reshape(TILES, 128), points, anchors, probes, trans_low, couple_low, trans_top, couple_top)


def solution(mesh):
    placed = (
        P("probe", "leaf"),
        P("leaf"),
        P(None, "leaf"),
        P(None, "leaf"),
        P("leaf", None, None, None),
        P("leaf", None, None, None),
        P(),
        P(),
    )
    return jax.shard_map(
        body, mesh=mesh, in_specs=placed, out_specs=P("probe", "leaf"), check_vma=False
    )
```

```python
import functools

import jax
import jax.numpy as jnp
from jax import lax
from jax.experimental import pallas as pl
from jax.experimental.pallas import tpu as pltpu
from jax.sharding import PartitionSpec as P

LEAF = 512
R = 128
PRB = 16
L_DEV = 4
PTS = 2048
N = 64
BLK = PTS // N
TILES = PTS // 128
SHARPNESS = 2.0
OUTPUT_SCALE = 0.25
NOISE_VAR = 0.5
MESH = pl.DeviceIdType.MESH
F32 = jnp.float32
BF16 = jnp.bfloat16
I32 = jnp.int32


def dot(a, b):
    return jnp.dot(a, b, preferred_element_type=F32)


def dot_nt(a, b):
    return lax.dot_general(a, b, (((1,), (1,)), ((), ())), preferred_element_type=F32)


def split(v):
    hi = v.astype(BF16)
    lo = (v - hi.astype(F32)).astype(BF16)
    return hi, lo


def pair(v):
    hi, lo = split(v)
    return jnp.concatenate([hi, lo], axis=0)


def fold(r):
    return r[:PRB] + r[PRB:]


def iota(shape, dim):
    return lax.broadcasted_iota(I32, shape, dim)


def swap_blocks(tile):
    lane = iota((8, 128), 1)
    row = iota((8, 128), 0)
    v0, v1 = tile[:8], tile[8:]
    low = lane < 64
    a0 = jnp.where(low, v0, pltpu.roll(v1, 64, 1))
    a1 = jnp.where(low, pltpu.roll(v0, 64, 1), v1)
    lane_bit = (lane >> 5) & 1
    same = (row >> 2) == lane_bit
    outs = []
    for a in (a0, a1):
        y = pltpu.roll(a, 4, 0)
        moved = jnp.where(lane_bit == 1, pltpu.roll(y, 32, 1), pltpu.roll(y, 96, 1))
        outs.append(jnp.where(same, a, moved))
    return outs


def gather_tile(source, index_row):
    index = jnp.broadcast_to(index_row, (8, 128))
    lane = index & 127
    tile = index >> 7
    out0 = jnp.zeros((8, 128), F32)
    out1 = jnp.zeros((8, 128), F32)
    for s in range(TILES):
        v = source(s)
        here = tile == s
        g0 = jnp.take_along_axis(v[:8], lane, axis=1, mode="promise_in_bounds")
        g1 = jnp.take_along_axis(v[8:], lane, axis=1, mode="promise_in_bounds")
        out0 = jnp.where(here, g0, out0)
        out1 = jnp.where(here, g1, out1)
    return jnp.concatenate([out0, out1], axis=0)


def near_order(v):
    return v + (v // 2) * (1 - 2 * (v % 2))


def by_lane_block(rows):
    block = iota((1, 128), 1) >> 5
    out = rows[3]
    for b in (2, 1, 0):
        out = jnp.where(block == b, rows[b], out)
    return out


def kernel(
    perm_h, points_h, anchors_h, probes_h, tl_h, cl_h, tt_h, ct_h,
    out_v,
    perm_v, points_v, anchors_v, probes_v, tl_v, cl_v,
    e0_v, e1_v, e2_v, e3_v, e4_v, ct_v, cs_v,
    slot_v, inv_v, asked_v, back_v,
    ptst_v, dhi_v, dlo_v, bhi_v, blo_v,
    x_v, x2_v, y_v, near_v,
    idx_s, idx_r, a_s, a_r, b_s, b_r,
    q0_v, q1_v, q2_v, q3_v, q4_v, q5_v,
    load_sem, send_sem, recv_sem, quad_sem,
):
    me = lax.axis_index("leaf")
    group = me // 8
    pos = me % 8

    def quad(k):
        along_z = ((me // 4) % 4 + near_order(k // 4)) % 4
        along_x = (me // 16 + near_order(k % 4)) % 4
        return along_x * 4 + along_z

    loads = [
        pltpu.make_async_copy(perm_h, perm_v, load_sem.at[0]),
        pltpu.make_async_copy(points_h, points_v.at[pl.ds(0, 3)], load_sem.at[1]),
        pltpu.make_async_copy(anchors_h, anchors_v, load_sem.at[2]),
        pltpu.make_async_copy(probes_h, probes_v, load_sem.at[3]),
        pltpu.make_async_copy(tl_h.at[0], tl_v, load_sem.at[4]),
        pltpu.make_async_copy(cl_h.at[0], cl_v, load_sem.at[5]),
        pltpu.make_async_copy(tt_h.at[pl.ds(group * 8, 8)], e0_v, load_sem.at[6]),
        pltpu.make_async_copy(tt_h.at[pl.ds(64 + group * 4, 4)], e1_v, load_sem.at[7]),
        pltpu.make_async_copy(tt_h.at[pl.ds(96 + group * 2, 2)], e2_v, load_sem.at[8]),
        pltpu.make_async_copy(tt_h.at[pl.ds(112, 8)], e3_v, load_sem.at[9]),
        pltpu.make_async_copy(tt_h.at[pl.ds(120, 4)], e4_v, load_sem.at[10]),
    ]
    for t, start in enumerate((0, 32, 48, 56, 60, 62)):
        loads.append(
            pltpu.make_async_copy(
                ct_h.at[pl.ds(start + me // (2 << t), 1)], ct_v.at[pl.ds(t, 1)], load_sem.at[11 + t]
            )
        )
    for copy in loads:
        copy.start()

    barrier = pltpu.get_barrier_semaphore()

    @pl.loop(1, N)
    def _(k):
        pl.semaphore_signal(barrier, inc=1, device_id={"leaf": (me + k) % N}, device_id_type=MESH)

    def remote(src, dst, which, peer, landed=None):
        return pltpu.make_async_remote_copy(
            src_ref=src, dst_ref=dst, send_sem=send_sem.at[which],
            recv_sem=recv_sem.at[which] if landed is None else landed,
            device_id={"leaf": peer}, device_id_type=MESH,
        )

    def send_quad(k, s_ref, r_ref, which):
        o = quad(k)
        for h in range(4):
            peer = 4 * o + h

            def start():
                remote(s_ref.at[peer], r_ref.at[me], which, peer, quad_sem.at[which, me // 4]).start()

            if isinstance(k, int) and k == 0:
                pl.when(peer != me)(start)
            else:
                start()

    def await_quad(k, s_ref, r_ref, which):
        count = 3 if isinstance(k, int) and k == 0 else 4
        o = quad(k)
        at = pl.ds(0, count)
        remote(s_ref.at[at], r_ref.at[at], which, me, quad_sem.at[which, o]).wait_recv()
        return o

    def sent_all(s_ref, r_ref, which):
        at = pl.ds(0, N - 1)
        remote(s_ref.at[at], r_ref.at[at], which, me).wait_send()

    loads[0].wait()
    row64 = iota((N, 128), 0)
    lane1 = iota((1, 128), 1)
    ones = []
    for b in range(TILES):
        home = perm_v[b : b + 1, :] >> 11
        ones.append((row64 == home).astype(F32))
    before = (iota((128, 128), 0) < iota((128, 128), 1)).astype(BF16)
    counter = jnp.concatenate([before, jnp.ones((128, 128), BF16)], axis=1)
    counts = dot(jnp.concatenate(ones, axis=0).astype(BF16), counter)
    base = jnp.zeros((N, 128), F32)
    found = jnp.zeros((4 * N, 128), F32)
    row128 = iota((128, 128), 0) & (BLK - 1)
    for b in range(TILES):
        entry = perm_v[b : b + 1, :]
        one = ones[b]
        rank = jnp.sum(one * (counts[N * b : N * (b + 1), :128] + base), axis=0, keepdims=True)
        base = base + counts[N * b : N * (b + 1), 128:]
        rank = rank.astype(I32)
        slot_v[b : b + 1, :] = (entry >> 11) * BLK + rank
        offset = entry & (PTS - 1)
        left = jnp.concatenate(
            [
                one * (offset >> 8).astype(F32),
                one * (offset & 255).astype(F32),
                one * float(b),
                one * lane1.astype(F32),
            ],
            axis=0,
        ).astype(BF16)
        right = (row128 == rank).astype(F32).astype(BF16)
        found = found + dot_nt(left, right)
    wanted = (found[:N] * 256.0 + found[N : 2 * N]).astype(I32)
    places = (found[2 * N : 3 * N] * 128.0 + found[3 * N :]).astype(I32)
    for h in range(N):
        idx_s[h] = wanted[h : h + 1, :]
    for o in range(TILES):
        inv_v[o : o + 1, :] = by_lane_block([places[4 * o + b : 4 * o + b + 1, :] for b in range(4)])

    loads[1].wait()
    loads[2].wait()
    for b in range(TILES):
        ptst_v[128 * b : 128 * (b + 1), :] = jnp.transpose(points_v[:, 128 * b : 128 * (b + 1)])

    rows = 64

    @pl.loop(0, PTS // rows)
    def _(i):
        at = pl.ds(pl.multiple_of(i * rows, rows), rows)
        leaf = i // (LEAF // rows)
        total = None
        for c in range(3):
            left = ptst_v[at, c : c + 1]
            right = anchors_v[c : c + 1, pl.ds(pl.multiple_of(leaf * R, R), R)]
            differ = left - right
            total = differ * differ if total is None else total + differ * differ
        hi, lo = split(jnp.exp(-SHARPNESS * total))
        bhi_v[at, :] = hi
        blo_v[at, :] = lo

    pl.semaphore_wait(barrier, N - 1)

    @pl.loop(0, TILES - 1)
    def _(i):
        send_quad(TILES - 1 - i, idx_s, idx_r, 0)

    send_quad(0, idx_s, idx_r, 0)
    idx_r[me] = idx_s[me]

    drows = 32

    def dense(leaf):
        @pl.loop(0, LEAF // drows)
        def _(i):
            at = pl.ds(pl.multiple_of(leaf * LEAF + i * drows, drows), drows)
            total = None
            for c in range(3):
                left = ptst_v[at, c : c + 1]
                right = points_v[c : c + 1, leaf * LEAF : (leaf + 1) * LEAF]
                differ = left - right
                total = differ * differ if total is None else total + differ * differ
            hi, lo = split(jnp.exp(-SHARPNESS * total))
            dhi_v[at, :] = hi
            dlo_v[at, :] = lo

    dense(0)
    loads[3].wait()

    def send_tile(tile, k, s_ref, r_ref, which):
        o = quad(k)
        halves = swap_blocks(tile)
        for h in range(4):
            s_ref[4 * o + h] = halves[h // 2][4 * (h % 2) : 4 * (h % 2) + 4]
        send_quad(k, s_ref, r_ref, which)

    def take_quads(s_ref, r_ref, which, slots, out):
        def take(k):
            o = await_quad(k, s_ref, r_ref, which)
            source = swap_blocks(jnp.concatenate([r_ref[4 * o + h] for h in range(4)], axis=0))
            for j in range(TILES):
                index = jnp.broadcast_to(slots[j : j + 1, :], (8, 128))
                lane = index & 127
                here = (index >> 7) == o
                for v in range(2):
                    at = (slice(8 * v, 8 * v + 8), slice(128 * j, 128 * (j + 1)))
                    got = jnp.take_along_axis(source[v], lane, axis=1, mode="promise_in_bounds")
                    out[at] = jnp.where(here, got, 0.0 if isinstance(k, int) else out[at])

        r_ref[me] = s_ref[me]
        take(0)

        @pl.loop(1, TILES)
        def _(k):
            take(k)

    def pick(k):
        o = await_quad(k, idx_s, idx_r, 0)
        asked = by_lane_block([idx_r[4 * o + b] for b in range(4)])
        asked_v[o] = asked
        tile = gather_tile(lambda s: probes_v[:, 128 * s : 128 * (s + 1)], asked)
        send_tile(tile, k, a_s, a_r, 1)

    pick(0)

    @pl.loop(1, TILES)
    def _(k):
        pick(k)

    dense(1)

    found = jnp.zeros((2 * TILES, 128), F32)
    row16 = iota((TILES, 128), 0)
    row128 = iota((128, 128), 0)
    for o in range(TILES):
        asked = asked_v[o]
        one = (row16 == (asked >> 7)).astype(F32)
        left = jnp.concatenate([one * float(o), one * lane1.astype(F32)], axis=0).astype(BF16)
        right = (row128 == (asked & 127)).astype(F32).astype(BF16)
        found = found + dot_nt(left, right)
    back_v[...] = (found[:TILES] * 128.0 + found[TILES:]).astype(I32)

    for copy in loads[4:]:
        copy.wait()
    for t in range(6):
        mat = ct_v[t].astype(F32)
        odd = (me // (1 << t)) % 2
        cs_v[t] = jnp.where(odd == 1, jnp.transpose(mat), mat).astype(BF16)

    take_quads(a_s, a_r, 1, slot_v, x_v)
    for o in range(TILES):
        at = slice(128 * o, 128 * (o + 1))
        x2_v[:, at] = pair(x_v[:, at])

    def up(children, transfers):
        lhs = pair(jnp.concatenate(children, axis=1))
        return fold(dot(lhs, transfers.reshape(2 * R, R)))

    leaves = []
    for i in range(L_DEV):
        x2 = x2_v[:, LEAF * i : LEAF * (i + 1)]
        at = slice(LEAF * i, LEAF * (i + 1))
        leaves.append(fold(dot(x2, bhi_v[at, :])) + dot(x2[:PRB], blo_v[at, :]))
    mids = [up(leaves[2 * n : 2 * n + 2], tl_v[2 * n : 2 * n + 2]) for n in range(2)]
    q0_v[pos] = up(mids, tl_v[4:6])

    @pl.loop(1, 8)
    def _(k):
        peer = group * 8 + (pos + k) % 8
        remote(q0_v.at[pos], q0_v.at[pos], 3, peer).start()

    def near(i):
        x2 = x2_v[:, LEAF * i : LEAF * (i + 1)]
        at = slice(LEAF * i, LEAF * (i + 1))
        near_v[:, at] = fold(dot(x2, dhi_v[at, :])) + dot(x2[:PRB], dlo_v[at, :])

    dense(2)
    near(0)
    remote(q0_v.at[pl.ds(0, 7)], q0_v.at[pl.ds(0, 7)], 3, me).wait()
    for n in range(4):
        q1_v[n] = up([q0_v[2 * n], q0_v[2 * n + 1]], e0_v[2 * n : 2 * n + 2])
    for n in range(2):
        q2_v[n] = up([q1_v[2 * n], q1_v[2 * n + 1]], e1_v[2 * n : 2 * n + 2])
    q3_v[group] = up([q2_v[0], q2_v[1]], e2_v[...])

    @pl.loop(1, 8)
    def _(k):
        peer = ((group + k) % 8) * 8 + pos
        remote(q3_v.at[group], q3_v.at[group], 4, peer).start()

    dense(3)
    near(1)
    near(2)
    near(3)
    remote(q3_v.at[pl.ds(0, 7)], q3_v.at[pl.ds(0, 7)], 4, me).wait()
    for n in range(4):
        q4_v[n] = up([q3_v[2 * n], q3_v[2 * n + 1]], e3_v[2 * n : 2 * n + 2])
    for n in range(2):
        q5_v[n] = up([q4_v[2 * n], q4_v[2 * n + 1]], e4_v[2 * n : 2 * n + 2])

    def other(index):
        return index + 1 - 2 * (index % 2)

    def coupled(q, matrix):
        return fold(dot(pair(q), matrix))

    def down(g, matrix):
        return fold(dot_nt(pair(g), matrix))

    g = coupled(q5_v[other(group // 4)], cs_v[5])
    g = coupled(q4_v[other(group // 2)], cs_v[4]) + down(g, e4_v[group // 2])
    g = coupled(q3_v[other(group)], cs_v[3]) + down(g, e3_v[group])
    g = coupled(q2_v[other(pos // 4)], cs_v[2]) + down(g, e2_v[pos // 4])
    g = coupled(q1_v[other(pos // 2)], cs_v[1]) + down(g, e1_v[pos // 2])
    g = coupled(q0_v[other(pos)], cs_v[0]) + down(g, e0_v[pos])

    def both_down(q_even, q_odd, coupling, g, e_even, e_odd):
        even = fold(dot(pair(q_odd), coupling)) + down(g, e_even)
        odd = fold(dot_nt(pair(q_even), coupling)) + down(g, e_odd)
        return even, odd

    g_mids = both_down(mids[0], mids[1], cl_v[2], g, tl_v[4], tl_v[5])
    for n in range(2):
        g_leaves = both_down(
            leaves[2 * n], leaves[2 * n + 1], cl_v[n], g_mids[n], tl_v[2 * n], tl_v[2 * n + 1]
        )
        for s in range(2):
            i = 2 * n + s
            at = slice(LEAF * i, LEAF * (i + 1))
            hi, lo = split(g_leaves[s])
            both = jnp.concatenate([hi, lo], axis=0)
            far = fold(dot_nt(both, bhi_v[at, :])) + dot_nt(hi, blo_v[at, :])
            y = OUTPUT_SCALE * (near_v[:, at] + far) + NOISE_VAR * x_v[:, at]
            for b in range(4):
                y_v[4 * i + b] = y[:, 128 * b : 128 * (b + 1)]

    def give(k):
        tile = gather_tile(lambda s: y_v[s], inv_v[pl.ds(quad(k), 1), :])
        send_tile(tile, k, b_s, b_r, 2)

    @pl.loop(0, TILES - 1)
    def _(i):
        give(TILES - 1 - i)

    give(0)
    take_quads(b_s, b_r, 2, back_v, out_v)
    sent_all(idx_s, idx_r, 0)
    sent_all(a_s, a_r, 1)
    sent_all(b_s, b_r, 2)


def body(probes, perm, points, anchors, trans_low, couple_low, trans_top, couple_top):
    vmem = pltpu.VMEM
    dma = pltpu.SemaphoreType.DMA
    return pl.pallas_call(
        kernel,
        out_shape=jax.ShapeDtypeStruct((PRB, PTS), F32),
        in_specs=[pl.BlockSpec(memory_space=pl.ANY)] * 8,
        out_specs=pl.BlockSpec(memory_space=pltpu.VMEM),
        scratch_shapes=[
            vmem((TILES, 128), I32),
            vmem((8, PTS), F32),
            vmem((3, L_DEV * R), F32),
            vmem((PRB, PTS), F32),
            vmem((6, R, R), BF16),
            vmem((3, R, R), BF16),
            vmem((8, R, R), BF16),
            vmem((4, R, R), BF16),
            vmem((2, R, R), BF16),
            vmem((8, R, R), BF16),
            vmem((4, R, R), BF16),
            vmem((6, R, R), BF16),
            vmem((6, R, R), BF16),
            vmem((TILES, 128), I32),
            vmem((TILES, 128), I32),
            vmem((TILES, 1, 128), I32),
            vmem((TILES, 128), I32),
            vmem((PTS, 8), F32),
            vmem((PTS, LEAF), BF16),
            vmem((PTS, LEAF), BF16),
            vmem((PTS, R), BF16),
            vmem((PTS, R), BF16),
            vmem((PRB, PTS), F32),
            vmem((2 * PRB, PTS), BF16),
            vmem((TILES, PRB, 128), F32),
            vmem((PRB, PTS), F32),
            vmem((N, 1, 128), I32),
            vmem((N, 1, 128), I32),
            vmem((N, 4, 128), F32),
            vmem((N, 4, 128), F32),
            vmem((N, 4, 128), F32),
            vmem((N, 4, 128), F32),
            vmem((8, PRB, R), F32),
            vmem((4, PRB, R), F32),
            vmem((2, PRB, R), F32),
            vmem((8, PRB, R), F32),
            vmem((4, PRB, R), F32),
            vmem((2, PRB, R), F32),
            dma((17,)),
            dma((5,)),
            dma((5,)),
            dma((3, TILES)),
        ],
        compiler_params=pltpu.CompilerParams(
            collective_id=0, has_side_effects=True, vmem_limit_bytes=56 * 1024 * 1024
        ),
        name="hss_product",
    )(perm.reshape(TILES, 128), points, anchors, probes, trans_low, couple_low, trans_top, couple_top)


def solution(mesh):
    placed = (
        P("probe", "leaf"),
        P("leaf"),
        P(None, "leaf"),
        P(None, "leaf"),
        P("leaf", None, None, None),
        P("leaf", None, None, None),
        P(),
        P(),
    )
    return jax.shard_map(
        body, mesh=mesh, in_specs=placed, out_specs=P("probe", "leaf"), check_vma=False
    )
```

```python
import functools

import jax
import jax.numpy as jnp
from jax import lax
from jax.experimental import pallas as pl
from jax.experimental.pallas import tpu as pltpu
from jax.sharding import PartitionSpec as P

LEAF = 512
R = 128
PRB = 16
L_DEV = 4
PTS = 2048
N = 64
BLK = PTS // N
TILES = PTS // 128
SHARPNESS = 2.0
OUTPUT_SCALE = 0.25
NOISE_VAR = 0.5
BATCHES = ((0, 8), (8, 16))
JB = 4
SB = 8
MESH = pl.DeviceIdType.MESH
F32 = jnp.float32
BF16 = jnp.bfloat16
I32 = jnp.int32


def dot(a, b):
    return jnp.dot(a, b, preferred_element_type=F32)


def dot_nt(a, b):
    return lax.dot_general(a, b, (((1,), (1,)), ((), ())), preferred_element_type=F32)


def split(v):
    hi = v.astype(BF16)
    lo = (v - hi.astype(F32)).astype(BF16)
    return hi, lo


def pair(v):
    hi, lo = split(v)
    return jnp.concatenate([hi, lo], axis=0)


def fold(r):
    return r[:PRB] + r[PRB:]


def iota(shape, dim):
    return lax.broadcasted_iota(I32, shape, dim)


def swap_blocks(tile):
    lane = iota((8, 128), 1)
    row = iota((8, 128), 0)
    v0, v1 = tile[:8], tile[8:]
    low = lane < 64
    a0 = jnp.where(low, v0, pltpu.roll(v1, 64, 1))
    a1 = jnp.where(low, pltpu.roll(v0, 64, 1), v1)
    lane_bit = (lane >> 5) & 1
    same = (row >> 2) == lane_bit
    outs = []
    for a in (a0, a1):
        y = pltpu.roll(a, 4, 0)
        moved = jnp.where(lane_bit == 1, pltpu.roll(y, 32, 1), pltpu.roll(y, 96, 1))
        outs.append(jnp.where(same, a, moved))
    return outs


def gather_tile(source, index_row):
    index = jnp.broadcast_to(index_row, (8, 128))
    lane = index & 127
    tile = index >> 7
    out0 = jnp.zeros((8, 128), F32)
    out1 = jnp.zeros((8, 128), F32)
    for s in range(TILES):
        v = source(s)
        here = tile == s
        g0 = jnp.take_along_axis(v[:8], lane, axis=1, mode="promise_in_bounds")
        g1 = jnp.take_along_axis(v[8:], lane, axis=1, mode="promise_in_bounds")
        out0 = jnp.where(here, g0, out0)
        out1 = jnp.where(here, g1, out1)
    return jnp.concatenate([out0, out1], axis=0)


def near_order(v):
    return v + (v // 2) * (1 - 2 * (v % 2))


def by_lane_block(rows):
    block = iota((1, 128), 1) >> 5
    out = rows[3]
    for b in (2, 1, 0):
        out = jnp.where(block == b, rows[b], out)
    return out


def kernel(
    perm_h, points_h, anchors_h, probes_h, tl_h, cl_h, tt_h, ct_h,
    out_v,
    perm_v, points_v, anchors_v, probes_v, tl_v, cl_v,
    e0_v, e1_v, e2_v, e3_v, e4_v, ct_v, cs_v,
    slot_v, inv_v, asked_v, back_v,
    ptst_v, dhi_v, dlo_v, bhi_v, blo_v,
    x_v, x2_v, xs_v, y_v, near_v,
    idx_s, idx_r, a_s, a_r, b_s, b_r,
    q0_v, q1_v, q2_v, q3_v, q4_v, q5_v,
    load_sem, send_sem, recv_sem, quad_sem,
):
    me = lax.axis_index("leaf")
    group = me // 8
    pos = me % 8

    def quad(k):
        along_z = ((me // 4) % 4 + near_order(k // 4)) % 4
        along_x = (me // 16 + near_order(k % 4)) % 4
        return along_x * 4 + along_z

    loads = [
        pltpu.make_async_copy(perm_h, perm_v, load_sem.at[0]),
        pltpu.make_async_copy(points_h, points_v.at[pl.ds(0, 3)], load_sem.at[1]),
        pltpu.make_async_copy(anchors_h, anchors_v, load_sem.at[2]),
        pltpu.make_async_copy(probes_h, probes_v, load_sem.at[3]),
        pltpu.make_async_copy(tl_h.at[0], tl_v, load_sem.at[4]),
        pltpu.make_async_copy(cl_h.at[0], cl_v, load_sem.at[5]),
        pltpu.make_async_copy(tt_h.at[pl.ds(group * 8, 8)], e0_v, load_sem.at[6]),
        pltpu.make_async_copy(tt_h.at[pl.ds(64 + group * 4, 4)], e1_v, load_sem.at[7]),
        pltpu.make_async_copy(tt_h.at[pl.ds(96 + group * 2, 2)], e2_v, load_sem.at[8]),
        pltpu.make_async_copy(tt_h.at[pl.ds(112, 8)], e3_v, load_sem.at[9]),
        pltpu.make_async_copy(tt_h.at[pl.ds(120, 4)], e4_v, load_sem.at[10]),
    ]
    for t, start in enumerate((0, 32, 48, 56, 60, 62)):
        loads.append(
            pltpu.make_async_copy(
                ct_h.at[pl.ds(start + me // (2 << t), 1)], ct_v.at[pl.ds(t, 1)], load_sem.at[11 + t]
            )
        )
    for copy in loads:
        copy.start()

    barrier = pltpu.get_barrier_semaphore()

    @pl.loop(1, N)
    def _(k):
        pl.semaphore_signal(barrier, inc=1, device_id={"leaf": (me + k) % N}, device_id_type=MESH)

    def remote(src, dst, which, peer, landed=None):
        return pltpu.make_async_remote_copy(
            src_ref=src, dst_ref=dst, send_sem=send_sem.at[which],
            recv_sem=recv_sem.at[which] if landed is None else landed,
            device_id={"leaf": peer}, device_id_type=MESH,
        )

    def send_quad(k, s_ref, r_ref, which):
        o = quad(k)
        for h in range(4):
            peer = 4 * o + h

            def start():
                remote(s_ref.at[peer], r_ref.at[me], which, peer, quad_sem.at[which, me // 4]).start()

            if isinstance(k, int) and k == 0:
                pl.when(peer != me)(start)
            else:
                start()

    def await_quad(k, s_ref, r_ref, which):
        count = 3 if isinstance(k, int) and k == 0 else 4
        o = quad(k)
        at = pl.ds(0, count)
        remote(s_ref.at[at], r_ref.at[at], which, me, quad_sem.at[which, o]).wait_recv()
        return o

    def sent_all(s_ref, r_ref, which):
        at = pl.ds(0, N - 1)
        remote(s_ref.at[at], r_ref.at[at], which, me).wait_send()

    loads[0].wait()
    row64 = iota((N, 128), 0)
    lane1 = iota((1, 128), 1)
    ones = []
    for b in range(TILES):
        home = perm_v[b : b + 1, :] >> 11
        ones.append((row64 == home).astype(F32))
    before = (iota((128, 128), 0) < iota((128, 128), 1)).astype(BF16)
    counter = jnp.concatenate([before, jnp.ones((128, 128), BF16)], axis=1)
    counts = dot(jnp.concatenate(ones, axis=0).astype(BF16), counter)
    base = jnp.zeros((N, 128), F32)
    found = jnp.zeros((4 * N, 128), F32)
    row128 = iota((128, 128), 0) & (BLK - 1)
    for b in range(TILES):
        entry = perm_v[b : b + 1, :]
        one = ones[b]
        rank = jnp.sum(one * (counts[N * b : N * (b + 1), :128] + base), axis=0, keepdims=True)
        base = base + counts[N * b : N * (b + 1), 128:]
        rank = rank.astype(I32)
        slot_v[b] = (entry >> 11) * BLK + rank
        offset = entry & (PTS - 1)
        left = jnp.concatenate(
            [
                one * (offset >> 8).astype(F32),
                one * (offset & 255).astype(F32),
                one * float(b),
                one * lane1.astype(F32),
            ],
            axis=0,
        ).astype(BF16)
        right = (row128 == rank).astype(F32).astype(BF16)
        found = found + dot_nt(left, right)
    wanted = (found[:N] * 256.0 + found[N : 2 * N]).astype(I32)
    places = (found[2 * N : 3 * N] * 128.0 + found[3 * N :]).astype(I32)
    for h in range(N):
        idx_s[h] = wanted[h : h + 1, :]
    for o in range(TILES):
        inv_v[o] = by_lane_block([places[4 * o + b : 4 * o + b + 1, :] for b in range(4)])

    loads[1].wait()
    loads[2].wait()
    for b in range(TILES):
        ptst_v[128 * b : 128 * (b + 1), :] = jnp.transpose(points_v[:, 128 * b : 128 * (b + 1)])

    rows = 64

    @pl.loop(0, PTS // rows)
    def _(i):
        at = pl.ds(pl.multiple_of(i * rows, rows), rows)
        leaf = i // (LEAF // rows)
        total = None
        for c in range(3):
            left = ptst_v[at, c : c + 1]
            right = anchors_v[c : c + 1, pl.ds(pl.multiple_of(leaf * R, R), R)]
            differ = left - right
            total = differ * differ if total is None else total + differ * differ
        hi, lo = split(jnp.exp(-SHARPNESS * total))
        bhi_v[at, :] = hi
        blo_v[at, :] = lo

    pl.semaphore_wait(barrier, N - 1)

    @pl.loop(0, TILES - 1)
    def _(i):
        send_quad(TILES - 1 - i, idx_s, idx_r, 0)

    send_quad(0, idx_s, idx_r, 0)
    idx_r[me] = idx_s[me]

    drows = 32

    def dense(leaf):
        @pl.loop(0, LEAF // drows)
        def _(i):
            at = pl.ds(pl.multiple_of(leaf * LEAF + i * drows, drows), drows)
            total = None
            for c in range(3):
                left = ptst_v[at, c : c + 1]
                right = points_v[c : c + 1, leaf * LEAF : (leaf + 1) * LEAF]
                differ = left - right
                total = differ * differ if total is None else total + differ * differ
            hi, lo = split(jnp.exp(-SHARPNESS * total))
            dhi_v[at, :] = hi
            dlo_v[at, :] = lo

    dense(0)
    loads[3].wait()

    def send_tiles(tiles, ks, s_ref, r_ref, which):
        for tile, k in zip(tiles, ks):
            o = quad(k)
            halves = swap_blocks(tile)
            for h in range(4):
                s_ref[4 * o + h] = halves[h // 2][4 * (h % 2) : 4 * (h % 2) + 4]
        for k in ks:
            send_quad(k, s_ref, r_ref, which)

    def take_quads(s_ref, r_ref, which, slots, out):
        r_ref[me] = s_ref[me]
        for first, last in BATCHES:
            ks = range(first, last)
            homes = [await_quad(k, s_ref, r_ref, which) for k in ks]
            for k, o in zip(ks, homes):
                both = swap_blocks(jnp.concatenate([r_ref[4 * o + h] for h in range(4)], axis=0))
                xs_v[k] = jnp.concatenate(both, axis=0)

            @pl.loop(0, TILES // JB)
            def _(i):
                for u in range(JB):
                    j = i * JB + u
                    index = jnp.broadcast_to(slots[j], (8, 128))
                    lane = index & 127
                    tile = index >> 7
                    got = [out[j, 8 * v : 8 * v + 8] if first else jnp.zeros((8, 128), F32) for v in range(2)]
                    for k, o in zip(ks, homes):
                        here = tile == o
                        for v in range(2):
                            part = jnp.take_along_axis(
                                xs_v[k, 8 * v : 8 * v + 8], lane, axis=1, mode="promise_in_bounds"
                            )
                            got[v] = jnp.where(here, part, got[v])
                    for v in range(2):
                        out[j, 8 * v : 8 * v + 8] = got[v]

    def pick(ks):
        tiles = []
        for k in ks:
            o = await_quad(k, idx_s, idx_r, 0)
            asked = by_lane_block([idx_r[4 * o + b] for b in range(4)])
            asked_v[o] = asked
            tiles.append(gather_tile(lambda s: probes_v[:, 128 * s : 128 * (s + 1)], asked))
        send_tiles(tiles, ks, a_s, a_r, 1)

    pick(list(range(SB)))

    @pl.loop(1, TILES // SB)
    def _(i):
        pick([SB * i + u for u in range(SB)])

    dense(1)

    found = jnp.zeros((2 * TILES, 128), F32)
    row16 = iota((TILES, 128), 0)
    row128 = iota((128, 128), 0)
    for o in range(TILES):
        asked = asked_v[o]
        one = (row16 == (asked >> 7)).astype(F32)
        left = jnp.concatenate([one * float(o), one * lane1.astype(F32)], axis=0).astype(BF16)
        right = (row128 == (asked & 127)).astype(F32).astype(BF16)
        found = found + dot_nt(left, right)
    back = (found[:TILES] * 128.0 + found[TILES:]).astype(I32)
    for o in range(TILES):
        back_v[o] = back[o : o + 1, :]

    for copy in loads[4:]:
        copy.wait()
    for t in range(6):
        mat = ct_v[t].astype(F32)
        odd = (me // (1 << t)) % 2
        cs_v[t] = jnp.where(odd == 1, jnp.transpose(mat), mat).astype(BF16)

    take_quads(a_s, a_r, 1, slot_v, x_v)
    for o in range(TILES):
        x2_v[:, 128 * o : 128 * (o + 1)] = pair(x_v[o])

    def up(children, transfers):
        lhs = pair(jnp.concatenate(children, axis=1))
        return fold(dot(lhs, transfers.reshape(2 * R, R)))

    leaves = []
    for i in range(L_DEV):
        x2 = x2_v[:, LEAF * i : LEAF * (i + 1)]
        at = slice(LEAF * i, LEAF * (i + 1))
        leaves.append(fold(dot(x2, bhi_v[at, :])) + dot(x2[:PRB], blo_v[at, :]))
    mids = [up(leaves[2 * n : 2 * n + 2], tl_v[2 * n : 2 * n + 2]) for n in range(2)]
    q0_v[pos] = up(mids, tl_v[4:6])

    @pl.loop(1, 8)
    def _(k):
        peer = group * 8 + (pos + k) % 8
        remote(q0_v.at[pos], q0_v.at[pos], 3, peer).start()

    def near(i):
        x2 = x2_v[:, LEAF * i : LEAF * (i + 1)]
        at = slice(LEAF * i, LEAF * (i + 1))
        near_v[:, at] = fold(dot(x2, dhi_v[at, :])) + dot(x2[:PRB], dlo_v[at, :])

    dense(2)
    near(0)
    remote(q0_v.at[pl.ds(0, 7)], q0_v.at[pl.ds(0, 7)], 3, me).wait()
    for n in range(4):
        q1_v[n] = up([q0_v[2 * n], q0_v[2 * n + 1]], e0_v[2 * n : 2 * n + 2])
    for n in range(2):
        q2_v[n] = up([q1_v[2 * n], q1_v[2 * n + 1]], e1_v[2 * n : 2 * n + 2])
    q3_v[group] = up([q2_v[0], q2_v[1]], e2_v[...])

    @pl.loop(1, 8)
    def _(k):
        peer = ((group + k) % 8) * 8 + pos
        remote(q3_v.at[group], q3_v.at[group], 4, peer).start()

    dense(3)
    near(1)
    near(2)
    near(3)
    remote(q3_v.at[pl.ds(0, 7)], q3_v.at[pl.ds(0, 7)], 4, me).wait()
    for n in range(4):
        q4_v[n] = up([q3_v[2 * n], q3_v[2 * n + 1]], e3_v[2 * n : 2 * n + 2])
    for n in range(2):
        q5_v[n] = up([q4_v[2 * n], q4_v[2 * n + 1]], e4_v[2 * n : 2 * n + 2])

    def other(index):
        return index + 1 - 2 * (index % 2)

    def coupled(q, matrix):
        return fold(dot(pair(q), matrix))

    def down(g, matrix):
        return fold(dot_nt(pair(g), matrix))

    g = coupled(q5_v[other(group // 4)], cs_v[5])
    g = coupled(q4_v[other(group // 2)], cs_v[4]) + down(g, e4_v[group // 2])
    g = coupled(q3_v[other(group)], cs_v[3]) + down(g, e3_v[group])
    g = coupled(q2_v[other(pos // 4)], cs_v[2]) + down(g, e2_v[pos // 4])
    g = coupled(q1_v[other(pos // 2)], cs_v[1]) + down(g, e1_v[pos // 2])
    g = coupled(q0_v[other(pos)], cs_v[0]) + down(g, e0_v[pos])

    def both_down(q_even, q_odd, coupling, g, e_even, e_odd):
        even = fold(dot(pair(q_odd), coupling)) + down(g, e_even)
        odd = fold(dot_nt(pair(q_even), coupling)) + down(g, e_odd)
        return even, odd

    g_mids = both_down(mids[0], mids[1], cl_v[2], g, tl_v[4], tl_v[5])
    for n in range(2):
        g_leaves = both_down(
            leaves[2 * n], leaves[2 * n + 1], cl_v[n], g_mids[n], tl_v[2 * n], tl_v[2 * n + 1]
        )
        for s in range(2):
            i = 2 * n + s
            at = slice(LEAF * i, LEAF * (i + 1))
            hi, lo = split(g_leaves[s])
            both = jnp.concatenate([hi, lo], axis=0)
            far = fold(dot_nt(both, bhi_v[at, :])) + dot_nt(hi, blo_v[at, :])
            y = OUTPUT_SCALE * (near_v[:, at] + far)
            for b in range(4):
                y_v[4 * i + b] = y[:, 128 * b : 128 * (b + 1)] + NOISE_VAR * x_v[4 * i + b]

    def give(ks):
        tiles = [gather_tile(lambda s: y_v[s], inv_v[quad(k)]) for k in ks]
        send_tiles(tiles, ks, b_s, b_r, 2)

    @pl.loop(0, TILES // SB - 1)
    def _(i):
        give([TILES - 1 - SB * i - u for u in range(SB)])

    give(list(range(SB)))
    take_quads(b_s, b_r, 2, back_v, y_v)
    for j in range(TILES):
        out_v[:, 128 * j : 128 * (j + 1)] = y_v[j]
    sent_all(idx_s, idx_r, 0)
    sent_all(a_s, a_r, 1)
    sent_all(b_s, b_r, 2)


def body(probes, perm, points, anchors, trans_low, couple_low, trans_top, couple_top):
    vmem = pltpu.VMEM
    dma = pltpu.SemaphoreType.DMA
    return pl.pallas_call(
        kernel,
        out_shape=jax.ShapeDtypeStruct((PRB, PTS), F32),
        in_specs=[pl.BlockSpec(memory_space=pl.ANY)] * 8,
        out_specs=pl.BlockSpec(memory_space=pltpu.VMEM),
        scratch_shapes=[
            vmem((TILES, 128), I32),
            vmem((8, PTS), F32),
            vmem((3, L_DEV * R), F32),
            vmem((PRB, PTS), F32),
            vmem((6, R, R), BF16),
            vmem((3, R, R), BF16),
            vmem((8, R, R), BF16),
            vmem((4, R, R), BF16),
            vmem((2, R, R), BF16),
            vmem((8, R, R), BF16),
            vmem((4, R, R), BF16),
            vmem((6, R, R), BF16),
            vmem((6, R, R), BF16),
            vmem((TILES, 1, 128), I32),
            vmem((TILES, 1, 128), I32),
            vmem((TILES, 1, 128), I32),
            vmem((TILES, 1, 128), I32),
            vmem((PTS, 8), F32),
            vmem((PTS, LEAF), BF16),
            vmem((PTS, LEAF), BF16),
            vmem((PTS, R), BF16),
            vmem((PTS, R), BF16),
            vmem((TILES, PRB, 128), F32),
            vmem((2 * PRB, PTS), BF16),
            vmem((TILES, PRB, 128), F32),
            vmem((TILES, PRB, 128), F32),
            vmem((PRB, PTS), F32),
            vmem((N, 1, 128), I32),
            vmem((N, 1, 128), I32),
            vmem((N, 4, 128), F32),
            vmem((N, 4, 128), F32),
            vmem((N, 4, 128), F32),
            vmem((N, 4, 128), F32),
            vmem((8, PRB, R), F32),
            vmem((4, PRB, R), F32),
            vmem((2, PRB, R), F32),
            vmem((8, PRB, R), F32),
            vmem((4, PRB, R), F32),
            vmem((2, PRB, R), F32),
            dma((17,)),
            dma((5,)),
            dma((5,)),
            dma((3, TILES)),
        ],
        compiler_params=pltpu.CompilerParams(
            collective_id=0, has_side_effects=True, vmem_limit_bytes=56 * 1024 * 1024
        ),
        name="hss_product",
    )(perm.reshape(TILES, 128), points, anchors, probes, trans_low, couple_low, trans_top, couple_top)


def solution(mesh):
    placed = (
        P("probe", "leaf"),
        P("leaf"),
        P(None, "leaf"),
        P(None, "leaf"),
        P("leaf", None, None, None),
        P("leaf", None, None, None),
        P(),
        P(),
    )
    return jax.shard_map(
        body, mesh=mesh, in_specs=placed, out_specs=P("probe", "leaf"), check_vma=False
    )
```

```python
import functools

import jax
import jax.numpy as jnp
from jax import lax
from jax.experimental import pallas as pl
from jax.experimental.pallas import tpu as pltpu
from jax.sharding import PartitionSpec as P

LEAF = 512
R = 128
PRB = 16
L_DEV = 4
PTS = 2048
N = 64
BLK = PTS // N
TILES = PTS // 128
SHARPNESS = 2.0
LOG2_E = 1.4426950408889634
OUTPUT_SCALE = 0.25
NOISE_VAR = 0.5
BATCHES = ((0, 8), (8, 16))
JB = 4
SB = 8
PB = 4
MESH = pl.DeviceIdType.MESH
F32 = jnp.float32
BF16 = jnp.bfloat16
I32 = jnp.int32


def dot(a, b):
    return jnp.dot(a, b, preferred_element_type=F32)


def dot_nt(a, b):
    return lax.dot_general(a, b, (((1,), (1,)), ((), ())), preferred_element_type=F32)


def split(v):
    hi = v.astype(BF16)
    lo = (v - hi.astype(F32)).astype(BF16)
    return hi, lo


def pair(v):
    hi, lo = split(v)
    return jnp.concatenate([hi, lo], axis=0)


def fold(r):
    return r[:PRB] + r[PRB:]


def fold_lanes(r):
    return r[:, :R] + r[:, R:]


def times_exact(pieces, matrix):
    r = dot(jnp.concatenate(pieces, axis=0), matrix)
    return split(r[:R] + r[R:])


def exact_times(matrix, pieces):
    return split(fold_lanes(dot(matrix, jnp.concatenate(pieces, axis=1))))


def exact_times_turned(matrix, pieces):
    return split(fold_lanes(dot_nt(matrix, jnp.concatenate(pieces, axis=0))))


def iota(shape, dim):
    return lax.broadcasted_iota(I32, shape, dim)


def swap_blocks(tile):
    lane = iota((8, 128), 1)
    row = iota((8, 128), 0)
    v0, v1 = tile[:8], tile[8:]
    low = lane < 64
    a0 = jnp.where(low, v0, pltpu.roll(v1, 64, 1))
    a1 = jnp.where(low, pltpu.roll(v0, 64, 1), v1)
    lane_bit = (lane >> 5) & 1
    same = (row >> 2) == lane_bit
    outs = []
    for a in (a0, a1):
        y = pltpu.roll(a, 4, 0)
        moved = jnp.where(lane_bit == 1, pltpu.roll(y, 32, 1), pltpu.roll(y, 96, 1))
        outs.append(jnp.where(same, a, moved))
    return outs


def gather_tile(source, index_row):
    index = jnp.broadcast_to(index_row, (8, 128))
    lane = index & 127
    tile = index >> 7
    out0 = jnp.zeros((8, 128), F32)
    out1 = jnp.zeros((8, 128), F32)
    for s in range(TILES):
        v = source(s)
        here = tile == s
        g0 = jnp.take_along_axis(v[:8], lane, axis=1, mode="promise_in_bounds")
        g1 = jnp.take_along_axis(v[8:], lane, axis=1, mode="promise_in_bounds")
        out0 = jnp.where(here, g0, out0)
        out1 = jnp.where(here, g1, out1)
    return jnp.concatenate([out0, out1], axis=0)


def near_order(v):
    return v + (v // 2) * (1 - 2 * (v % 2))


def by_lane_block(rows):
    block = iota((1, 128), 1) >> 5
    out = rows[3]
    for b in (2, 1, 0):
        out = jnp.where(block == b, rows[b], out)
    return out


def kernel(
    perm_h, points_h, anchors_h, probes_h, tl_h, cl_h, tt_h, ct_h,
    out_v,
    perm_v, points_v, anchors_v, probes_v, tl_v, cl_v,
    e0_v, e1_v, e2_v, e3_v, e4_v, ct_v, cs_v,
    slot_v, inv_v, asked_v, back_v,
    ptst_v, dhi_v, dlo_v, bhi_v, blo_v, uhi_v, ulo_v, f1_v, whi_v, wlo_v,
    x_v, x2_v, xs_v, y_v,
    idx_s, idx_r, a_s, a_r, b_s, b_r,
    q0_v, q1_v, q2_v, q3_v, q4_v,
    load_sem, send_sem, recv_sem, quad_sem,
):
    me = lax.axis_index("leaf")
    group = me // 8
    pos = me % 8

    def quad(k):
        along_z = ((me // 4) % 4 + near_order(k // 4)) % 4
        along_x = (me // 16 + near_order(k % 4)) % 4
        return along_x * 4 + along_z

    loads = [
        pltpu.make_async_copy(perm_h, perm_v, load_sem.at[0]),
        pltpu.make_async_copy(points_h, points_v.at[pl.ds(0, 3)], load_sem.at[1]),
        pltpu.make_async_copy(anchors_h, anchors_v, load_sem.at[2]),
        pltpu.make_async_copy(probes_h, probes_v, load_sem.at[3]),
        pltpu.make_async_copy(tl_h.at[0], tl_v, load_sem.at[4]),
        pltpu.make_async_copy(cl_h.at[0], cl_v, load_sem.at[5]),
        pltpu.make_async_copy(tt_h.at[pl.ds(group * 8, 8)], e0_v, load_sem.at[6]),
        pltpu.make_async_copy(tt_h.at[pl.ds(64 + group * 4, 4)], e1_v, load_sem.at[7]),
        pltpu.make_async_copy(tt_h.at[pl.ds(96 + group * 2, 2)], e2_v, load_sem.at[8]),
        pltpu.make_async_copy(tt_h.at[pl.ds(112, 8)], e3_v, load_sem.at[9]),
        pltpu.make_async_copy(tt_h.at[pl.ds(120, 4)], e4_v, load_sem.at[10]),
    ]
    for t, start in enumerate((0, 32, 48, 56, 60, 62)):
        loads.append(
            pltpu.make_async_copy(
                ct_h.at[pl.ds(start + me // (2 << t), 1)], ct_v.at[pl.ds(t, 1)], load_sem.at[11 + t]
            )
        )
    for copy in loads:
        copy.start()

    barrier = pltpu.get_barrier_semaphore()

    @pl.loop(1, N)
    def _(k):
        pl.semaphore_signal(barrier, inc=1, device_id={"leaf": (me + k) % N}, device_id_type=MESH)

    def remote(src, dst, which, peer, landed=None):
        return pltpu.make_async_remote_copy(
            src_ref=src, dst_ref=dst, send_sem=send_sem.at[which],
            recv_sem=recv_sem.at[which] if landed is None else landed,
            device_id={"leaf": peer}, device_id_type=MESH,
        )

    def send_quad(k, s_ref, r_ref, which):
        o = quad(k)
        for h in range(4):
            peer = 4 * o + h

            def start():
                remote(s_ref.at[peer], r_ref.at[me], which, peer, quad_sem.at[which, me // 4]).start()

            if isinstance(k, int) and k == 0:
                pl.when(peer != me)(start)
            else:
                start()

    def await_quad(k, s_ref, r_ref, which):
        count = 3 if isinstance(k, int) and k == 0 else 4
        o = quad(k)
        at = pl.ds(0, count)
        remote(s_ref.at[at], r_ref.at[at], which, me, quad_sem.at[which, o]).wait_recv()
        return o

    def sent_all(s_ref, r_ref, which):
        at = pl.ds(0, N - 1)
        remote(s_ref.at[at], r_ref.at[at], which, me).wait_send()

    loads[0].wait()
    row64 = iota((N, 128), 0)
    lane1 = iota((1, 128), 1)
    ones = []
    for b in range(TILES):
        home = perm_v[b : b + 1, :] >> 11
        ones.append((row64 == home).astype(F32))
    before = (iota((128, 128), 0) < iota((128, 128), 1)).astype(BF16)
    counter = jnp.concatenate([before, jnp.ones((128, 128), BF16)], axis=1)
    counts = dot(jnp.concatenate(ones, axis=0).astype(BF16), counter)
    base = jnp.zeros((N, 128), F32)
    found = jnp.zeros((4 * N, 128), F32)
    row128 = iota((128, 128), 0) & (BLK - 1)
    for b in range(TILES):
        entry = perm_v[b : b + 1, :]
        one = ones[b]
        rank = jnp.sum(one * (counts[N * b : N * (b + 1), :128] + base), axis=0, keepdims=True)
        base = base + counts[N * b : N * (b + 1), 128:]
        rank = rank.astype(I32)
        slot_v[b] = (entry >> 11) * BLK + rank
        offset = entry & (PTS - 1)
        left = jnp.concatenate(
            [
                one * (offset >> 8).astype(F32),
                one * (offset & 255).astype(F32),
                one * float(b),
                one * lane1.astype(F32),
            ],
            axis=0,
        ).astype(BF16)
        right = (row128 == rank).astype(F32).astype(BF16)
        found = found + dot_nt(left, right)
    wanted = (found[:N] * 256.0 + found[N : 2 * N]).astype(I32)
    places = (found[2 * N : 3 * N] * 128.0 + found[3 * N :]).astype(I32)
    for h in range(N):
        idx_s[h] = wanted[h : h + 1, :]
    for o in range(TILES):
        inv_v[o] = by_lane_block([places[4 * o + b : 4 * o + b + 1, :] for b in range(4)])

    pl.semaphore_wait(barrier, N - 1)

    @pl.loop(0, TILES - 1)
    def _(i):
        send_quad(TILES - 1 - i, idx_s, idx_r, 0)

    send_quad(0, idx_s, idx_r, 0)
    idx_r[me] = idx_s[me]

    loads[1].wait()
    loads[2].wait()
    for b in range(TILES):
        ptst_v[128 * b : 128 * (b + 1), :] = jnp.transpose(points_v[:, 128 * b : 128 * (b + 1)])

    rows = 64

    @pl.loop(0, PTS // rows)
    def _(i):
        at = pl.ds(pl.multiple_of(i * rows, rows), rows)
        leaf = i // (LEAF // rows)
        total = None
        for c in range(3):
            left = ptst_v[at, c : c + 1]
            right = anchors_v[c : c + 1, pl.ds(pl.multiple_of(leaf * R, R), R)]
            differ = left - right
            total = differ * differ if total is None else total + differ * differ
        hi, lo = split(jnp.exp2((-SHARPNESS * LOG2_E) * total))
        bhi_v[at, :] = hi
        blo_v[at, :] = lo

    drows = 32

    def dense(leaf):
        @pl.loop(0, LEAF // drows)
        def _(i):
            at = pl.ds(pl.multiple_of(leaf * LEAF + i * drows, drows), drows)
            total = None
            for c in range(3):
                left = ptst_v[at, c : c + 1]
                right = points_v[c : c + 1, leaf * LEAF : (leaf + 1) * LEAF]
                differ = left - right
                total = differ * differ if total is None else total + differ * differ
            hi, lo = split(jnp.exp2((-SHARPNESS * LOG2_E) * total))
            dhi_v[at, :] = hi
            dlo_v[at, :] = lo

    loads[3].wait()

    def send_tiles(tiles, ks, s_ref, r_ref, which):
        for tile, k in zip(tiles, ks):
            o = quad(k)
            halves = swap_blocks(tile)
            for h in range(4):
                s_ref[4 * o + h] = halves[h // 2][4 * (h % 2) : 4 * (h % 2) + 4]
        for k in ks:
            send_quad(k, s_ref, r_ref, which)

    def take_quads(s_ref, r_ref, which, slots, out):
        r_ref[me] = s_ref[me]
        for first, last in BATCHES:
            ks = range(first, last)
            homes = [await_quad(k, s_ref, r_ref, which) for k in ks]
            for k, o in zip(ks, homes):
                both = swap_blocks(jnp.concatenate([r_ref[4 * o + h] for h in range(4)], axis=0))
                xs_v[k] = jnp.concatenate(both, axis=0)

            @pl.loop(0, TILES // JB)
            def _(i):
                for u in range(JB):
                    j = i * JB + u
                    index = jnp.broadcast_to(slots[j], (8, 128))
                    lane = index & 127
                    tile = index >> 7
                    got = [out[j, 8 * v : 8 * v + 8] if first else jnp.zeros((8, 128), F32) for v in range(2)]
                    for k, o in zip(ks, homes):
                        here = tile == o
                        for v in range(2):
                            part = jnp.take_along_axis(
                                xs_v[k, 8 * v : 8 * v + 8], lane, axis=1, mode="promise_in_bounds"
                            )
                            got[v] = jnp.where(here, part, got[v])
                    for v in range(2):
                        out[j, 8 * v : 8 * v + 8] = got[v]

    def pick(ks):
        tiles = []
        for k in ks:
            o = await_quad(k, idx_s, idx_r, 0)
            asked = by_lane_block([idx_r[4 * o + b] for b in range(4)])
            asked_v[o] = asked
            tiles.append(gather_tile(lambda s: probes_v[:, 128 * s : 128 * (s + 1)], asked))
        send_tiles(tiles, ks, a_s, a_r, 1)

    pick(list(range(PB)))

    @pl.loop(1, TILES // PB)
    def _(i):
        pick([PB * i + u for u in range(PB)])


    found = jnp.zeros((2 * TILES, 128), F32)
    row16 = iota((TILES, 128), 0)
    row128 = iota((128, 128), 0)
    for o in range(TILES):
        asked = asked_v[o]
        one = (row16 == (asked >> 7)).astype(F32)
        left = jnp.concatenate([one * float(o), one * lane1.astype(F32)], axis=0).astype(BF16)
        right = (row128 == (asked & 127)).astype(F32).astype(BF16)
        found = found + dot_nt(left, right)
    back = (found[:TILES] * 128.0 + found[TILES:]).astype(I32)
    for o in range(TILES):
        back_v[o] = back[o : o + 1, :]

    for copy in loads[5:]:
        copy.wait()
    for t in range(6):
        mat = ct_v[t].astype(F32)
        odd = (me // (1 << t)) % 2
        cs_v[t] = jnp.where(odd == 1, jnp.transpose(mat), mat).astype(BF16)

    def other(index):
        return index + 1 - 2 * (index % 2)

    far_half = other(group // 4)
    path = split(dot(e0_v[pos], e1_v[pos // 2]))
    f1_v[0], f1_v[1] = path
    path = times_exact(path, e2_v[pos // 4])
    links = [exact_times_turned(cs_v[3], path)]
    path = times_exact(path, e3_v[group])
    links.append(exact_times_turned(cs_v[4], path))
    path = times_exact(path, e4_v[group // 2])
    last = exact_times_turned(cs_v[5], path)
    for n in range(2):
        links.append(exact_times(e4_v[2 * far_half + n], last))
    for n in range(4):
        whi_v[R * n : R * (n + 1), :] = links[n][0]
        wlo_v[R * n : R * (n + 1), :] = links[n][1]
    loads[4].wait()
    for i in range(L_DEV):
        at = slice(LEAF * i, LEAF * (i + 1))
        hi, lo = split(dot(tl_v[i], tl_v[4 + i // 2]))
        both = fold_lanes(dot(bhi_v[at, :], jnp.concatenate([hi, lo], axis=1)))
        hi, lo = split(both + dot(blo_v[at, :], hi))
        uhi_v[at, :] = hi
        ulo_v[at, :] = lo


    take_quads(a_s, a_r, 1, slot_v, x_v)
    for o in range(TILES):
        x2_v[:, 128 * o : 128 * (o + 1)] = pair(x_v[o])

    def up(children, transfers):
        lhs = pair(jnp.concatenate(children, axis=1))
        return fold(dot(lhs, transfers.reshape(2 * R, R)))

    x2 = x2_v[...]
    q0_v[pos] = fold(dot(x2, uhi_v[...])) + dot(x2[:PRB], ulo_v[...])

    @pl.loop(1, 8)
    def _(k):
        peer = group * 8 + (pos + k) % 8
        remote(q0_v.at[pos], q0_v.at[pos], 3, peer).start()

    def near(i):
        x2 = x2_v[:, LEAF * i : LEAF * (i + 1)]
        at = slice(LEAF * i, LEAF * (i + 1))
        hi, lo = split(within[i])
        both = jnp.concatenate([hi, lo], axis=0)
        inner = fold(dot(x2, dhi_v[at, :])) + dot(x2[:PRB], dlo_v[at, :])
        inner = inner + fold(dot_nt(both, bhi_v[at, :])) + dot_nt(hi, blo_v[at, :])
        for b in range(4):
            y_v[4 * i + b] = OUTPUT_SCALE * inner[:, 128 * b : 128 * (b + 1)] + NOISE_VAR * x_v[4 * i + b]

    dense(0)
    dense(1)

    def coupled(q, matrix):
        return fold(dot(pair(q), matrix))

    def down(g, matrix):
        return fold(dot_nt(pair(g), matrix))

    leaves = []
    for i in range(L_DEV):
        x2 = x2_v[:, LEAF * i : LEAF * (i + 1)]
        at = slice(LEAF * i, LEAF * (i + 1))
        leaves.append(fold(dot(x2, bhi_v[at, :])) + dot(x2[:PRB], blo_v[at, :]))
    mids = [up(leaves[2 * n : 2 * n + 2], tl_v[2 * n : 2 * n + 2]) for n in range(2)]
    within_mids = [coupled(mids[1], cl_v[2]), down(mids[0], cl_v[2])]
    within = []
    for n in range(2):
        within.append(coupled(leaves[2 * n + 1], cl_v[n]) + down(within_mids[n], tl_v[2 * n]))
        within.append(down(leaves[2 * n], cl_v[n]) + down(within_mids[n], tl_v[2 * n + 1]))

    remote(q0_v.at[pl.ds(0, 7)], q0_v.at[pl.ds(0, 7)], 3, me).wait()
    for n in range(4):
        q1_v[n] = up([q0_v[2 * n], q0_v[2 * n + 1]], e0_v[2 * n : 2 * n + 2])
    for n in range(2):
        q2_v[n] = up([q1_v[2 * n], q1_v[2 * n + 1]], e1_v[2 * n : 2 * n + 2])
    q3_v[group] = up([q2_v[0], q2_v[1]], e2_v[...])

    @pl.loop(1, 8)
    def _(k):
        peer = ((group + k) % 8) * 8 + pos
        remote(q3_v.at[group], q3_v.at[group], 4, peer).start()

    part = coupled(q0_v[other(pos)], cs_v[0]) + down(coupled(q1_v[other(pos // 2)], cs_v[1]), e0_v[pos])
    hi, lo = split(coupled(q2_v[other(pos // 4)], cs_v[2]))
    both = jnp.concatenate([hi, lo], axis=0)
    part = part + fold(dot_nt(both, f1_v[0])) + dot_nt(hi, f1_v[1])
    dense(2)
    near(0)
    near(1)
    near(2)
    dense(3)
    near(3)
    remote(q3_v.at[pl.ds(0, 7)], q3_v.at[pl.ds(0, 7)], 4, me).wait()
    for n in range(4):
        q4_v[n] = up([q3_v[2 * n], q3_v[2 * n + 1]], e3_v[2 * n : 2 * n + 2])
    tops = [q3_v[other(group)], q4_v[other(group // 2)], q4_v[2 * far_half], q4_v[2 * far_half + 1]]
    hi, lo = split(jnp.concatenate(tops, axis=1))
    g = part + fold(dot(jnp.concatenate([hi, lo], axis=0), whi_v[...])) + dot(hi, wlo_v[...])
    hi, lo = split(g)
    far = fold(dot_nt(jnp.concatenate([hi, lo], axis=0), uhi_v[...])) + dot_nt(hi, ulo_v[...])
    for j in range(TILES):
        y_v[j] = y_v[j] + OUTPUT_SCALE * far[:, 128 * j : 128 * (j + 1)]

    def give(ks):
        tiles = [gather_tile(lambda s: y_v[s], inv_v[quad(k)]) for k in ks]
        send_tiles(tiles, ks, b_s, b_r, 2)

    @pl.loop(0, TILES // SB - 1)
    def _(i):
        give([TILES - 1 - SB * i - u for u in range(SB)])

    give(list(range(SB)))
    take_quads(b_s, b_r, 2, back_v, y_v)
    for j in range(TILES):
        out_v[:, 128 * j : 128 * (j + 1)] = y_v[j]
    sent_all(idx_s, idx_r, 0)
    sent_all(a_s, a_r, 1)
    sent_all(b_s, b_r, 2)


def body(probes, perm, points, anchors, trans_low, couple_low, trans_top, couple_top):
    vmem = pltpu.VMEM
    dma = pltpu.SemaphoreType.DMA
    return pl.pallas_call(
        kernel,
        out_shape=pltpu.VMEM((PRB, PTS), F32),
        in_specs=[pl.BlockSpec(memory_space=pl.ANY)] * 8,
        out_specs=pl.BlockSpec(memory_space=pltpu.VMEM),
        scratch_shapes=[
            vmem((TILES, 128), I32),
            vmem((8, PTS), F32),
            vmem((3, L_DEV * R), F32),
            vmem((PRB, PTS), F32),
            vmem((6, R, R), BF16),
            vmem((3, R, R), BF16),
            vmem((8, R, R), BF16),
            vmem((4, R, R), BF16),
            vmem((2, R, R), BF16),
            vmem((8, R, R), BF16),
            vmem((4, R, R), BF16),
            vmem((6, R, R), BF16),
            vmem((6, R, R), BF16),
            vmem((TILES, 1, 128), I32),
            vmem((TILES, 1, 128), I32),
            vmem((TILES, 1, 128), I32),
            vmem((TILES, 1, 128), I32),
            vmem((PTS, 8), F32),
            vmem((PTS, LEAF), BF16),
            vmem((PTS, LEAF), BF16),
            vmem((PTS, R), BF16),
            vmem((PTS, R), BF16),
            vmem((PTS, R), BF16),
            vmem((PTS, R), BF16),
            vmem((2, R, R), BF16),
            vmem((4 * R, R), BF16),
            vmem((4 * R, R), BF16),
            vmem((TILES, PRB, 128), F32),
            vmem((2 * PRB, PTS), BF16),
            vmem((TILES, PRB, 128), F32),
            vmem((TILES, PRB, 128), F32),
            vmem((N, 1, 128), I32),
            vmem((N, 1, 128), I32),
            vmem((N, 4, 128), F32),
            vmem((N, 4, 128), F32),
            vmem((N, 4, 128), F32),
            vmem((N, 4, 128), F32),
            vmem((8, PRB, R), F32),
            vmem((4, PRB, R), F32),
            vmem((2, PRB, R), F32),
            vmem((8, PRB, R), F32),
            vmem((4, PRB, R), F32),
            dma((17,)),
            dma((5,)),
            dma((5,)),
            dma((3, TILES)),
        ],
        compiler_params=pltpu.CompilerParams(
            collective_id=0, has_side_effects=True, vmem_limit_bytes=56 * 1024 * 1024
        ),
        name="hss_product",
    )(perm.reshape(TILES, 128), points, anchors, probes, trans_low, couple_low, trans_top, couple_top)


def solution(mesh):
    placed = (
        P("probe", "leaf"),
        P("leaf"),
        P(None, "leaf"),
        P(None, "leaf"),
        P("leaf", None, None, None),
        P("leaf", None, None, None),
        P(),
        P(),
    )
    return jax.shard_map(
        body, mesh=mesh, in_specs=placed, out_specs=P("probe", "leaf"), check_vma=False
    )
```

```python
import functools

import jax
import jax.numpy as jnp
from jax import lax
from jax.experimental import pallas as pl
from jax.experimental.pallas import tpu as pltpu
from jax.sharding import PartitionSpec as P

LEAF = 512
R = 128
PRB = 16
L_DEV = 4
PTS = 2048
N = 64
BLK = PTS // N
TILES = PTS // 128
SHARPNESS = 2.0
LOG2_E = 1.4426950408889634
OUTPUT_SCALE = 0.25
NOISE_VAR = 0.5
BATCHES = ((0, 8), (8, 16))
JB = 4
SB = 8
PB = 8
MESH = pl.DeviceIdType.MESH
F32 = jnp.float32
BF16 = jnp.bfloat16
I32 = jnp.int32


def dot(a, b):
    return jnp.dot(a, b, preferred_element_type=F32)


def dot_nt(a, b):
    return lax.dot_general(a, b, (((1,), (1,)), ((), ())), preferred_element_type=F32)


def split(v):
    hi = v.astype(BF16)
    lo = (v - hi.astype(F32)).astype(BF16)
    return hi, lo


def pair(v):
    hi, lo = split(v)
    return jnp.concatenate([hi, lo], axis=0)


def fold(r):
    return r[:PRB] + r[PRB:]


def fold_lanes(r):
    return r[:, :R] + r[:, R:]


def times_exact(pieces, matrix):
    r = dot(jnp.concatenate(pieces, axis=0), matrix)
    return split(r[:R] + r[R:])


def exact_times(matrix, pieces):
    return split(fold_lanes(dot(matrix, jnp.concatenate(pieces, axis=1))))


def exact_times_turned(matrix, pieces):
    return split(fold_lanes(dot_nt(matrix, jnp.concatenate(pieces, axis=0))))


def iota(shape, dim):
    return lax.broadcasted_iota(I32, shape, dim)


def swap_blocks(tile):
    lane = iota((8, 128), 1)
    row = iota((8, 128), 0)
    v0, v1 = tile[:8], tile[8:]
    low = lane < 64
    a0 = jnp.where(low, v0, pltpu.roll(v1, 64, 1))
    a1 = jnp.where(low, pltpu.roll(v0, 64, 1), v1)
    lane_bit = (lane >> 5) & 1
    same = (row >> 2) == lane_bit
    outs = []
    for a in (a0, a1):
        y = pltpu.roll(a, 4, 0)
        moved = jnp.where(lane_bit == 1, pltpu.roll(y, 32, 1), pltpu.roll(y, 96, 1))
        outs.append(jnp.where(same, a, moved))
    return outs


def gather_tile(source, index_row):
    index = jnp.broadcast_to(index_row, (8, 128))
    lane = index & 127
    tile = index >> 7
    out0 = jnp.zeros((8, 128), F32)
    out1 = jnp.zeros((8, 128), F32)
    for s in range(TILES):
        v = source(s)
        here = tile == s
        g0 = jnp.take_along_axis(v[:8], lane, axis=1, mode="promise_in_bounds")
        g1 = jnp.take_along_axis(v[8:], lane, axis=1, mode="promise_in_bounds")
        out0 = jnp.where(here, g0, out0)
        out1 = jnp.where(here, g1, out1)
    return jnp.concatenate([out0, out1], axis=0)


def near_order(v):
    return v + (v // 2) * (1 - 2 * (v % 2))


def by_lane_block(rows):
    block = iota((1, 128), 1) >> 5
    out = rows[3]
    for b in (2, 1, 0):
        out = jnp.where(block == b, rows[b], out)
    return out


def kernel(
    perm_h, points_h, anchors_h, probes_h, tl_h, cl_h, tt_h, ct_h,
    out_v,
    perm_v, points_v, anchors_v, probes_v, tl_v, cl_v,
    e0_v, e1_v, e2_v, e3_v, e4_v, ct_v, cs_v,
    slot_v, inv_v, asked_v, back_v,
    ptst_v, dhi_v, dlo_v, bhi_v, blo_v, uhi_v, ulo_v, f1_v, whi_v, wlo_v,
    x_v, x2_v, xs_v, y_v,
    idx_s, idx_r, a_s, a_r, b_s, b_r,
    q0_v, q1_v, q2_v, q3_v, q4_v,
    load_sem, send_sem, recv_sem, quad_sem,
):
    me = lax.axis_index("leaf")
    group = me // 8
    pos = me % 8

    def quad(k):
        along_z = ((me // 4) % 4 + near_order(k // 4)) % 4
        along_x = (me // 16 + near_order(k % 4)) % 4
        return along_x * 4 + along_z

    loads = [
        pltpu.make_async_copy(perm_h, perm_v, load_sem.at[0]),
        pltpu.make_async_copy(points_h, points_v.at[pl.ds(0, 3)], load_sem.at[1]),
        pltpu.make_async_copy(anchors_h, anchors_v, load_sem.at[2]),
        pltpu.make_async_copy(probes_h, probes_v, load_sem.at[3]),
        pltpu.make_async_copy(tl_h.at[0], tl_v, load_sem.at[4]),
        pltpu.make_async_copy(cl_h.at[0], cl_v, load_sem.at[5]),
        pltpu.make_async_copy(tt_h.at[pl.ds(group * 8, 8)], e0_v, load_sem.at[6]),
        pltpu.make_async_copy(tt_h.at[pl.ds(64 + group * 4, 4)], e1_v, load_sem.at[7]),
        pltpu.make_async_copy(tt_h.at[pl.ds(96 + group * 2, 2)], e2_v, load_sem.at[8]),
        pltpu.make_async_copy(tt_h.at[pl.ds(112, 8)], e3_v, load_sem.at[9]),
        pltpu.make_async_copy(tt_h.at[pl.ds(120, 4)], e4_v, load_sem.at[10]),
    ]
    for t, start in enumerate((0, 32, 48, 56, 60, 62)):
        loads.append(
            pltpu.make_async_copy(
                ct_h.at[pl.ds(start + me // (2 << t), 1)], ct_v.at[pl.ds(t, 1)], load_sem.at[11 + t]
            )
        )
    for copy in loads:
        copy.start()

    barrier = pltpu.get_barrier_semaphore()

    @pl.loop(1, N)
    def _(k):
        pl.semaphore_signal(barrier, inc=1, device_id={"leaf": (me + k) % N}, device_id_type=MESH)

    def remote(src, dst, which, peer, landed=None):
        return pltpu.make_async_remote_copy(
            src_ref=src, dst_ref=dst, send_sem=send_sem.at[which],
            recv_sem=recv_sem.at[which] if landed is None else landed,
            device_id={"leaf": peer}, device_id_type=MESH,
        )

    def send_quad(k, s_ref, r_ref, which):
        o = quad(k)
        for h in range(4):
            peer = 4 * o + h

            def start():
                remote(s_ref.at[peer], r_ref.at[me], which, peer, quad_sem.at[which, me // 4]).start()

            if isinstance(k, int) and k == 0:
                pl.when(peer != me)(start)
            else:
                start()

    def await_quad(k, s_ref, r_ref, which):
        count = 3 if isinstance(k, int) and k == 0 else 4
        o = quad(k)
        at = pl.ds(0, count)
        remote(s_ref.at[at], r_ref.at[at], which, me, quad_sem.at[which, o]).wait_recv()
        return o

    def sent_all(s_ref, r_ref, which):
        at = pl.ds(0, N - 1)
        remote(s_ref.at[at], r_ref.at[at], which, me).wait_send()

    loads[0].wait()
    row64 = iota((N, 128), 0)
    lane1 = iota((1, 128), 1)
    ones = []
    for b in range(TILES):
        home = perm_v[b : b + 1, :] >> 11
        ones.append((row64 == home).astype(F32))
    before = (iota((128, 128), 0) < iota((128, 128), 1)).astype(BF16)
    counter = jnp.concatenate([before, jnp.ones((128, 128), BF16)], axis=1)
    counts = dot(jnp.concatenate(ones, axis=0).astype(BF16), counter)
    base = jnp.zeros((N, 128), F32)
    found = jnp.zeros((4 * N, 128), F32)
    row128 = iota((128, 128), 0) & (BLK - 1)
    for b in range(TILES):
        entry = perm_v[b : b + 1, :]
        one = ones[b]
        rank = jnp.sum(one * (counts[N * b : N * (b + 1), :128] + base), axis=0, keepdims=True)
        base = base + counts[N * b : N * (b + 1), 128:]
        rank = rank.astype(I32)
        slot_v[b] = (entry >> 11) * BLK + rank
        offset = entry & (PTS - 1)
        left = jnp.concatenate(
            [
                one * (offset >> 8).astype(F32),
                one * (offset & 255).astype(F32),
                one * float(b),
                one * lane1.astype(F32),
            ],
            axis=0,
        ).astype(BF16)
        right = (row128 == rank).astype(F32).astype(BF16)
        found = found + dot_nt(left, right)
    wanted = (found[:N] * 256.0 + found[N : 2 * N]).astype(I32)
    places = (found[2 * N : 3 * N] * 128.0 + found[3 * N :]).astype(I32)
    for h in range(N):
        idx_s[h] = wanted[h : h + 1, :]
    for o in range(TILES):
        inv_v[o] = by_lane_block([places[4 * o + b : 4 * o + b + 1, :] for b in range(4)])

    pl.semaphore_wait(barrier, N - 1)

    @pl.loop(0, TILES - 1)
    def _(i):
        send_quad(TILES - 1 - i, idx_s, idx_r, 0)

    send_quad(0, idx_s, idx_r, 0)
    idx_r[me] = idx_s[me]

    loads[1].wait()
    loads[2].wait()
    for b in range(TILES):
        ptst_v[128 * b : 128 * (b + 1), :] = jnp.transpose(points_v[:, 128 * b : 128 * (b + 1)])

    rows = 256

    @pl.loop(0, PTS // rows)
    def _(i):
        at = pl.ds(pl.multiple_of(i * rows, rows), rows)
        leaf = i // (LEAF // rows)
        total = None
        for c in range(3):
            left = ptst_v[at, c : c + 1]
            right = anchors_v[c : c + 1, pl.ds(pl.multiple_of(leaf * R, R), R)]
            differ = left - right
            total = differ * differ if total is None else total + differ * differ
        hi, lo = split(jnp.exp2((-SHARPNESS * LOG2_E) * total))
        bhi_v[at, :] = hi
        blo_v[at, :] = lo

    drows = 128

    def dense(leaf):
        @pl.loop(0, LEAF // drows)
        def _(i):
            at = pl.ds(pl.multiple_of(leaf * LEAF + i * drows, drows), drows)
            total = None
            for c in range(3):
                left = ptst_v[at, c : c + 1]
                right = points_v[c : c + 1, leaf * LEAF : (leaf + 1) * LEAF]
                differ = left - right
                total = differ * differ if total is None else total + differ * differ
            hi, lo = split(jnp.exp2((-SHARPNESS * LOG2_E) * total))
            dhi_v[at, :] = hi
            dlo_v[at, :] = lo

    loads[3].wait()

    def send_tiles(tiles, ks, s_ref, r_ref, which):
        for tile, k in zip(tiles, ks):
            o = quad(k)
            halves = swap_blocks(tile)
            for h in range(4):
                s_ref[4 * o + h] = halves[h // 2][4 * (h % 2) : 4 * (h % 2) + 4]
        for k in ks:
            send_quad(k, s_ref, r_ref, which)

    def take_quads(s_ref, r_ref, which, slots, out):
        r_ref[me] = s_ref[me]
        for first, last in BATCHES:
            ks = range(first, last)
            homes = [await_quad(k, s_ref, r_ref, which) for k in ks]
            for k, o in zip(ks, homes):
                both = swap_blocks(jnp.concatenate([r_ref[4 * o + h] for h in range(4)], axis=0))
                xs_v[k] = jnp.concatenate(both, axis=0)

            @pl.loop(0, TILES // JB)
            def _(i):
                for u in range(JB):
                    j = i * JB + u
                    index = jnp.broadcast_to(slots[j], (8, 128))
                    lane = index & 127
                    tile = index >> 7
                    got = [out[j, 8 * v : 8 * v + 8] if first else jnp.zeros((8, 128), F32) for v in range(2)]
                    for k, o in zip(ks, homes):
                        here = tile == o
                        for v in range(2):
                            part = jnp.take_along_axis(
                                xs_v[k, 8 * v : 8 * v + 8], lane, axis=1, mode="promise_in_bounds"
                            )
                            got[v] = jnp.where(here, part, got[v])
                    for v in range(2):
                        out[j, 8 * v : 8 * v + 8] = got[v]

    def pick(ks):
        tiles = []
        for k in ks:
            o = await_quad(k, idx_s, idx_r, 0)
            asked = by_lane_block([idx_r[4 * o + b] for b in range(4)])
            asked_v[o] = asked
            tiles.append(gather_tile(lambda s: probes_v[:, 128 * s : 128 * (s + 1)], asked))
        send_tiles(tiles, ks, a_s, a_r, 1)

    pick(list(range(PB)))

    @pl.loop(1, TILES // PB)
    def _(i):
        pick([PB * i + u for u in range(PB)])


    found = jnp.zeros((2 * TILES, 128), F32)
    row16 = iota((TILES, 128), 0)
    row128 = iota((128, 128), 0)
    for o in range(TILES):
        asked = asked_v[o]
        one = (row16 == (asked >> 7)).astype(F32)
        left = jnp.concatenate([one * float(o), one * lane1.astype(F32)], axis=0).astype(BF16)
        right = (row128 == (asked & 127)).astype(F32).astype(BF16)
        found = found + dot_nt(left, right)
    back = (found[:TILES] * 128.0 + found[TILES:]).astype(I32)
    for o in range(TILES):
        back_v[o] = back[o : o + 1, :]

    for copy in loads[5:]:
        copy.wait()
    for t in range(6):
        mat = ct_v[t].astype(F32)
        odd = (me // (1 << t)) % 2
        cs_v[t] = jnp.where(odd == 1, jnp.transpose(mat), mat).astype(BF16)

    def other(index):
        return index + 1 - 2 * (index % 2)

    far_half = other(group // 4)
    path = split(dot(e0_v[pos], e1_v[pos // 2]))
    f1_v[0], f1_v[1] = path
    path = times_exact(path, e2_v[pos // 4])
    links = [exact_times_turned(cs_v[3], path)]
    path = times_exact(path, e3_v[group])
    links.append(exact_times_turned(cs_v[4], path))
    path = times_exact(path, e4_v[group // 2])
    last = exact_times_turned(cs_v[5], path)
    for n in range(2):
        links.append(exact_times(e4_v[2 * far_half + n], last))
    for n in range(4):
        whi_v[R * n : R * (n + 1), :] = links[n][0]
        wlo_v[R * n : R * (n + 1), :] = links[n][1]
    loads[4].wait()
    for i in range(L_DEV):
        at = slice(LEAF * i, LEAF * (i + 1))
        hi, lo = split(dot(tl_v[i], tl_v[4 + i // 2]))
        both = fold_lanes(dot(bhi_v[at, :], jnp.concatenate([hi, lo], axis=1)))
        hi, lo = split(both + dot(blo_v[at, :], hi))
        uhi_v[at, :] = hi
        ulo_v[at, :] = lo


    take_quads(a_s, a_r, 1, slot_v, x_v)
    for o in range(TILES):
        x2_v[:, 128 * o : 128 * (o + 1)] = pair(x_v[o])

    def up(children, transfers):
        lhs = pair(jnp.concatenate(children, axis=1))
        return fold(dot(lhs, transfers.reshape(2 * R, R)))

    x2 = x2_v[...]
    q0_v[pos] = fold(dot(x2, uhi_v[...])) + dot(x2[:PRB], ulo_v[...])

    @pl.loop(1, 8)
    def _(k):
        peer = group * 8 + (pos + k) % 8
        remote(q0_v.at[pos], q0_v.at[pos], 3, peer).start()

    def near(i):
        x2 = x2_v[:, LEAF * i : LEAF * (i + 1)]
        at = slice(LEAF * i, LEAF * (i + 1))
        hi, lo = split(within[i])
        both = jnp.concatenate([hi, lo], axis=0)
        inner = fold(dot(x2, dhi_v[at, :])) + dot(x2[:PRB], dlo_v[at, :])
        inner = inner + fold(dot_nt(both, bhi_v[at, :])) + dot_nt(hi, blo_v[at, :])
        for b in range(4):
            y_v[4 * i + b] = OUTPUT_SCALE * inner[:, 128 * b : 128 * (b + 1)] + NOISE_VAR * x_v[4 * i + b]

    dense(0)
    dense(1)

    def coupled(q, matrix):
        return fold(dot(pair(q), matrix))

    def down(g, matrix):
        return fold(dot_nt(pair(g), matrix))

    leaves = []
    for i in range(L_DEV):
        x2 = x2_v[:, LEAF * i : LEAF * (i + 1)]
        at = slice(LEAF * i, LEAF * (i + 1))
        leaves.append(fold(dot(x2, bhi_v[at, :])) + dot(x2[:PRB], blo_v[at, :]))
    mids = [up(leaves[2 * n : 2 * n + 2], tl_v[2 * n : 2 * n + 2]) for n in range(2)]
    within_mids = [coupled(mids[1], cl_v[2]), down(mids[0], cl_v[2])]
    within = []
    for n in range(2):
        within.append(coupled(leaves[2 * n + 1], cl_v[n]) + down(within_mids[n], tl_v[2 * n]))
        within.append(down(leaves[2 * n], cl_v[n]) + down(within_mids[n], tl_v[2 * n + 1]))

    remote(q0_v.at[pl.ds(0, 7)], q0_v.at[pl.ds(0, 7)], 3, me).wait()
    for n in range(4):
        q1_v[n] = up([q0_v[2 * n], q0_v[2 * n + 1]], e0_v[2 * n : 2 * n + 2])
    for n in range(2):
        q2_v[n] = up([q1_v[2 * n], q1_v[2 * n + 1]], e1_v[2 * n : 2 * n + 2])
    q3_v[group] = up([q2_v[0], q2_v[1]], e2_v[...])

    @pl.loop(1, 8)
    def _(k):
        peer = ((group + k) % 8) * 8 + pos
        remote(q3_v.at[group], q3_v.at[group], 4, peer).start()

    part = coupled(q0_v[other(pos)], cs_v[0]) + down(coupled(q1_v[other(pos // 2)], cs_v[1]), e0_v[pos])
    hi, lo = split(coupled(q2_v[other(pos // 4)], cs_v[2]))
    both = jnp.concatenate([hi, lo], axis=0)
    part = part + fold(dot_nt(both, f1_v[0])) + dot_nt(hi, f1_v[1])
    dense(2)
    near(0)
    near(1)
    near(2)
    dense(3)
    near(3)
    remote(q3_v.at[pl.ds(0, 7)], q3_v.at[pl.ds(0, 7)], 4, me).wait()
    for n in range(4):
        q4_v[n] = up([q3_v[2 * n], q3_v[2 * n + 1]], e3_v[2 * n : 2 * n + 2])
    tops = [q3_v[other(group)], q4_v[other(group // 2)], q4_v[2 * far_half], q4_v[2 * far_half + 1]]
    hi, lo = split(jnp.concatenate(tops, axis=1))
    g = part + fold(dot(jnp.concatenate([hi, lo], axis=0), whi_v[...])) + dot(hi, wlo_v[...])
    hi, lo = split(g)
    far = fold(dot_nt(jnp.concatenate([hi, lo], axis=0), uhi_v[...])) + dot_nt(hi, ulo_v[...])
    for j in range(TILES):
        y_v[j] = y_v[j] + OUTPUT_SCALE * far[:, 128 * j : 128 * (j + 1)]

    def give(ks):
        tiles = [gather_tile(lambda s: y_v[s], inv_v[quad(k)]) for k in ks]
        send_tiles(tiles, ks, b_s, b_r, 2)

    @pl.loop(0, TILES // SB - 1)
    def _(i):
        give([TILES - 1 - SB * i - u for u in range(SB)])

    give(list(range(SB)))
    take_quads(b_s, b_r, 2, back_v, y_v)
    for j in range(TILES):
        out_v[:, 128 * j : 128 * (j + 1)] = y_v[j]
    sent_all(idx_s, idx_r, 0)
    sent_all(a_s, a_r, 1)
    sent_all(b_s, b_r, 2)


def body(probes, perm, points, anchors, trans_low, couple_low, trans_top, couple_top):
    vmem = pltpu.VMEM
    dma = pltpu.SemaphoreType.DMA
    return pl.pallas_call(
        kernel,
        out_shape=pltpu.VMEM((PRB, PTS), F32),
        in_specs=[pl.BlockSpec(memory_space=pl.ANY)] * 8,
        out_specs=pl.BlockSpec(memory_space=pltpu.VMEM),
        scratch_shapes=[
            vmem((TILES, 128), I32),
            vmem((8, PTS), F32),
            vmem((3, L_DEV * R), F32),
            vmem((PRB, PTS), F32),
            vmem((6, R, R), BF16),
            vmem((3, R, R), BF16),
            vmem((8, R, R), BF16),
            vmem((4, R, R), BF16),
            vmem((2, R, R), BF16),
            vmem((8, R, R), BF16),
            vmem((4, R, R), BF16),
            vmem((6, R, R), BF16),
            vmem((6, R, R), BF16),
            vmem((TILES, 1, 128), I32),
            vmem((TILES, 1, 128), I32),
            vmem((TILES, 1, 128), I32),
            vmem((TILES, 1, 128), I32),
            vmem((PTS, 8), F32),
            vmem((PTS, LEAF), BF16),
            vmem((PTS, LEAF), BF16),
            vmem((PTS, R), BF16),
            vmem((PTS, R), BF16),
            vmem((PTS, R), BF16),
            vmem((PTS, R), BF16),
            vmem((2, R, R), BF16),
            vmem((4 * R, R), BF16),
            vmem((4 * R, R), BF16),
            vmem((TILES, PRB, 128), F32),
            vmem((2 * PRB, PTS), BF16),
            vmem((TILES, PRB, 128), F32),
            vmem((TILES, PRB, 128), F32),
            vmem((N, 1, 128), I32),
            vmem((N, 1, 128), I32),
            vmem((N, 4, 128), F32),
            vmem((N, 4, 128), F32),
            vmem((N, 4, 128), F32),
            vmem((N, 4, 128), F32),
            vmem((8, PRB, R), F32),
            vmem((4, PRB, R), F32),
            vmem((2, PRB, R), F32),
            vmem((8, PRB, R), F32),
            vmem((4, PRB, R), F32),
            dma((17,)),
            dma((5,)),
            dma((5,)),
            dma((3, TILES)),
        ],
        compiler_params=pltpu.CompilerParams(
            collective_id=0, has_side_effects=True, vmem_limit_bytes=56 * 1024 * 1024
        ),
        name="hss_product",
    )(perm.reshape(TILES, 128), points, anchors, probes, trans_low, couple_low, trans_top, couple_top)


def solution(mesh):
    placed = (
        P("probe", "leaf"),
        P("leaf"),
        P(None, "leaf"),
        P(None, "leaf"),
        P("leaf", None, None, None),
        P("leaf", None, None, None),
        P(),
        P(),
    )
    return jax.shard_map(
        body, mesh=mesh, in_specs=placed, out_specs=P("probe", "leaf"), check_vma=False
    )
```

```python
import functools

import jax
import jax.numpy as jnp
from jax import lax
from jax.experimental import pallas as pl
from jax.experimental.pallas import tpu as pltpu
from jax.sharding import PartitionSpec as P

LEAF = 512
R = 128
PRB = 16
L_DEV = 4
PTS = 2048
N = 64
BLK = PTS // N
TILES = PTS // 128
SHARPNESS = 2.0
LOG2_E = 1.4426950408889634
OUTPUT_SCALE = 0.25
NOISE_VAR = 0.5
BATCHES = ((0, 8), (8, 16))
JB = 4
SB = 8
PB = 8
MESH = pl.DeviceIdType.MESH
F32 = jnp.float32
BF16 = jnp.bfloat16
I32 = jnp.int32


def dot(a, b):
    return jnp.dot(a, b, preferred_element_type=F32)


def dot_nt(a, b):
    return lax.dot_general(a, b, (((1,), (1,)), ((), ())), preferred_element_type=F32)


def split(v):
    hi = v.astype(BF16)
    lo = (v - hi.astype(F32)).astype(BF16)
    return hi, lo


def pair(v):
    hi, lo = split(v)
    return jnp.concatenate([hi, lo], axis=0)


def fold(r):
    return r[:PRB] + r[PRB:]


def fold_lanes(r):
    return r[:, :R] + r[:, R:]


def times_exact(pieces, matrix):
    r = dot(jnp.concatenate(pieces, axis=0), matrix)
    return split(r[:R] + r[R:])


def exact_times(matrix, pieces):
    return split(fold_lanes(dot(matrix, jnp.concatenate(pieces, axis=1))))


def exact_times_turned(matrix, pieces):
    return split(fold_lanes(dot_nt(matrix, jnp.concatenate(pieces, axis=0))))


def iota(shape, dim):
    return lax.broadcasted_iota(I32, shape, dim)


def swap_blocks(tile):
    lane = iota((8, 128), 1)
    row = iota((8, 128), 0)
    v0, v1 = tile[:8], tile[8:]
    low = lane < 64
    a0 = jnp.where(low, v0, pltpu.roll(v1, 64, 1))
    a1 = jnp.where(low, pltpu.roll(v0, 64, 1), v1)
    lane_bit = (lane >> 5) & 1
    same = (row >> 2) == lane_bit
    outs = []
    for a in (a0, a1):
        y = pltpu.roll(a, 4, 0)
        moved = jnp.where(lane_bit == 1, pltpu.roll(y, 32, 1), pltpu.roll(y, 96, 1))
        outs.append(jnp.where(same, a, moved))
    return outs


def gather_tile(source, index_row):
    index = jnp.broadcast_to(index_row, (8, 128))
    lane = index & 127
    tile = index >> 7
    out0 = jnp.zeros((8, 128), F32)
    out1 = jnp.zeros((8, 128), F32)
    for s in range(TILES):
        v = source(s)
        here = tile == s
        g0 = jnp.take_along_axis(v[:8], lane, axis=1, mode="promise_in_bounds")
        g1 = jnp.take_along_axis(v[8:], lane, axis=1, mode="promise_in_bounds")
        out0 = jnp.where(here, g0, out0)
        out1 = jnp.where(here, g1, out1)
    return jnp.concatenate([out0, out1], axis=0)


def near_order(v):
    return v + (v // 2) * (1 - 2 * (v % 2))


def by_lane_block(rows):
    block = iota((1, 128), 1) >> 5
    out = rows[3]
    for b in (2, 1, 0):
        out = jnp.where(block == b, rows[b], out)
    return out


def kernel(
    perm_h, points_h, anchors_h, probes_h, tl_h, cl_h, tt_h, ct_h,
    out_v,
    perm_v, points_v, anchors_v, probes_v, tl_v, cl_v,
    e0_v, e1_v, e2_v, e3_v, e4_v, ct_v, cs_v,
    slot_v, inv_v, asked_v, back_v,
    ptst_v, dhi_v, dlo_v, bhi_v, blo_v, uhi_v, ulo_v, f1_v, whi_v, wlo_v,
    x_v, x2_v, xs_v, y_v,
    idx_s, idx_r, a_s, a_r, b_s, b_r,
    q0_v, q1_v, q2_v, q3_v, q4_v,
    load_sem, send_sem, recv_sem, quad_sem,
):
    me = lax.axis_index("leaf")
    group = me // 8
    pos = me % 8

    def quad(k):
        along_z = ((me // 4) % 4 + near_order(k // 4)) % 4
        along_x = (me // 16 + near_order(k % 4)) % 4
        return along_x * 4 + along_z

    loads = [
        pltpu.make_async_copy(perm_h, perm_v, load_sem.at[0]),
        pltpu.make_async_copy(points_h, points_v.at[pl.ds(0, 3)], load_sem.at[1]),
        pltpu.make_async_copy(anchors_h, anchors_v, load_sem.at[2]),
        pltpu.make_async_copy(probes_h, probes_v, load_sem.at[3]),
        pltpu.make_async_copy(tl_h.at[0], tl_v, load_sem.at[4]),
        pltpu.make_async_copy(cl_h.at[0], cl_v, load_sem.at[5]),
        pltpu.make_async_copy(tt_h.at[pl.ds(group * 8, 8)], e0_v, load_sem.at[6]),
        pltpu.make_async_copy(tt_h.at[pl.ds(64 + group * 4, 4)], e1_v, load_sem.at[7]),
        pltpu.make_async_copy(tt_h.at[pl.ds(96 + group * 2, 2)], e2_v, load_sem.at[8]),
        pltpu.make_async_copy(tt_h.at[pl.ds(112, 8)], e3_v, load_sem.at[9]),
        pltpu.make_async_copy(tt_h.at[pl.ds(120, 4)], e4_v, load_sem.at[10]),
    ]
    for t, start in enumerate((0, 32, 48, 56, 60, 62)):
        loads.append(
            pltpu.make_async_copy(
                ct_h.at[pl.ds(start + me // (2 << t), 1)], ct_v.at[pl.ds(t, 1)], load_sem.at[11 + t]
            )
        )
    for copy in loads:
        copy.start()

    barrier = pltpu.get_barrier_semaphore()

    def greet(peer):
        pl.semaphore_signal(barrier, inc=1, device_id={"leaf": peer}, device_id_type=MESH)

    @pl.loop(0, TILES - 1)
    def _(i):
        for h in range(4):
            greet(4 * quad(TILES - 1 - i) + h)

    for h in range(4):
        peer = 4 * quad(0) + h
        pl.when(peer != me)(functools.partial(greet, peer))


    def remote(src, dst, which, peer, landed=None):
        return pltpu.make_async_remote_copy(
            src_ref=src, dst_ref=dst, send_sem=send_sem.at[which],
            recv_sem=recv_sem.at[which] if landed is None else landed,
            device_id={"leaf": peer}, device_id_type=MESH,
        )

    def send_quad(k, s_ref, r_ref, which):
        o = quad(k)
        for h in range(4):
            peer = 4 * o + h

            def start():
                remote(s_ref.at[peer], r_ref.at[me], which, peer, quad_sem.at[which, me // 4]).start()

            if isinstance(k, int) and k == 0:
                pl.when(peer != me)(start)
            else:
                start()

    def await_quad(k, s_ref, r_ref, which):
        count = 3 if isinstance(k, int) and k == 0 else 4
        o = quad(k)
        at = pl.ds(0, count)
        remote(s_ref.at[at], r_ref.at[at], which, me, quad_sem.at[which, o]).wait_recv()
        return o

    def sent_all(s_ref, r_ref, which):
        at = pl.ds(0, N - 1)
        remote(s_ref.at[at], r_ref.at[at], which, me).wait_send()

    loads[0].wait()
    row64 = iota((N, 128), 0)
    lane1 = iota((1, 128), 1)
    ones = []
    for b in range(TILES):
        home = perm_v[b : b + 1, :] >> 11
        ones.append((row64 == home).astype(F32))
    before = (iota((128, 128), 0) < iota((128, 128), 1)).astype(BF16)
    counter = jnp.concatenate([before, jnp.ones((128, 128), BF16)], axis=1)
    counts = dot(jnp.concatenate(ones, axis=0).astype(BF16), counter)
    base = jnp.zeros((N, 128), F32)
    found = jnp.zeros((4 * N, 128), F32)
    row128 = iota((128, 128), 0) & (BLK - 1)
    for b in range(TILES):
        entry = perm_v[b : b + 1, :]
        one = ones[b]
        rank = jnp.sum(one * (counts[N * b : N * (b + 1), :128] + base), axis=0, keepdims=True)
        base = base + counts[N * b : N * (b + 1), 128:]
        rank = rank.astype(I32)
        slot_v[b] = (entry >> 11) * BLK + rank
        offset = entry & (PTS - 1)
        left = jnp.concatenate(
            [
                one * (offset >> 8).astype(F32),
                one * (offset & 255).astype(F32),
                one * float(b),
                one * lane1.astype(F32),
            ],
            axis=0,
        ).astype(BF16)
        right = (row128 == rank).astype(F32).astype(BF16)
        found = found + dot_nt(left, right)
    wanted = (found[:N] * 256.0 + found[N : 2 * N]).astype(I32)
    places = (found[2 * N : 3 * N] * 128.0 + found[3 * N :]).astype(I32)
    for h in range(N):
        idx_s[h] = wanted[h : h + 1, :]
    for o in range(TILES):
        inv_v[o] = by_lane_block([places[4 * o + b : 4 * o + b + 1, :] for b in range(4)])

    pl.semaphore_wait(barrier, N - 1)

    @pl.loop(0, TILES - 1)
    def _(i):
        send_quad(TILES - 1 - i, idx_s, idx_r, 0)

    send_quad(0, idx_s, idx_r, 0)
    idx_r[me] = idx_s[me]

    loads[1].wait()
    loads[2].wait()
    for b in range(TILES):
        ptst_v[128 * b : 128 * (b + 1), :] = jnp.transpose(points_v[:, 128 * b : 128 * (b + 1)])

    rows = 256

    @pl.loop(0, PTS // rows)
    def _(i):
        at = pl.ds(pl.multiple_of(i * rows, rows), rows)
        leaf = i // (LEAF // rows)
        total = None
        for c in range(3):
            left = ptst_v[at, c : c + 1]
            right = anchors_v[c : c + 1, pl.ds(pl.multiple_of(leaf * R, R), R)]
            differ = left - right
            total = differ * differ if total is None else total + differ * differ
        hi, lo = split(jnp.exp2((-SHARPNESS * LOG2_E) * total))
        bhi_v[at, :] = hi
        blo_v[at, :] = lo

    drows = 128

    def dense(leaf):
        @pl.loop(0, LEAF // drows)
        def _(i):
            at = pl.ds(pl.multiple_of(leaf * LEAF + i * drows, drows), drows)
            total = None
            for c in range(3):
                left = ptst_v[at, c : c + 1]
                right = points_v[c : c + 1, leaf * LEAF : (leaf + 1) * LEAF]
                differ = left - right
                total = differ * differ if total is None else total + differ * differ
            hi, lo = split(jnp.exp2((-SHARPNESS * LOG2_E) * total))
            dhi_v[at, :] = hi
            dlo_v[at, :] = lo

    loads[3].wait()

    def send_tiles(tiles, ks, s_ref, r_ref, which):
        for tile, k in zip(tiles, ks):
            o = quad(k)
            halves = swap_blocks(tile)
            for h in range(4):
                s_ref[4 * o + h] = halves[h // 2][4 * (h % 2) : 4 * (h % 2) + 4]
        for k in ks:
            send_quad(k, s_ref, r_ref, which)

    def take_quads(s_ref, r_ref, which, slots, out):
        r_ref[me] = s_ref[me]
        for first, last in BATCHES:
            ks = range(first, last)
            homes = [await_quad(k, s_ref, r_ref, which) for k in ks]
            for k, o in zip(ks, homes):
                both = swap_blocks(jnp.concatenate([r_ref[4 * o + h] for h in range(4)], axis=0))
                xs_v[k] = jnp.concatenate(both, axis=0)

            @pl.loop(0, TILES // JB)
            def _(i):
                for u in range(JB):
                    j = i * JB + u
                    index = jnp.broadcast_to(slots[j], (8, 128))
                    lane = index & 127
                    tile = index >> 7
                    got = [out[j, 8 * v : 8 * v + 8] if first else jnp.zeros((8, 128), F32) for v in range(2)]
                    for k, o in zip(ks, homes):
                        here = tile == o
                        for v in range(2):
                            part = jnp.take_along_axis(
                                xs_v[k, 8 * v : 8 * v + 8], lane, axis=1, mode="promise_in_bounds"
                            )
                            got[v] = jnp.where(here, part, got[v])
                    for v in range(2):
                        out[j, 8 * v : 8 * v + 8] = got[v]

    def pick(ks):
        tiles = []
        for k in ks:
            o = await_quad(k, idx_s, idx_r, 0)
            asked = by_lane_block([idx_r[4 * o + b] for b in range(4)])
            asked_v[o] = asked
            tiles.append(gather_tile(lambda s: probes_v[:, 128 * s : 128 * (s + 1)], asked))
        send_tiles(tiles, ks, a_s, a_r, 1)

    pick(list(range(PB)))

    @pl.loop(1, TILES // PB)
    def _(i):
        pick([PB * i + u for u in range(PB)])


    found = jnp.zeros((2 * TILES, 128), F32)
    row16 = iota((TILES, 128), 0)
    row128 = iota((128, 128), 0)
    for o in range(TILES):
        asked = asked_v[o]
        one = (row16 == (asked >> 7)).astype(F32)
        left = jnp.concatenate([one * float(o), one * lane1.astype(F32)], axis=0).astype(BF16)
        right = (row128 == (asked & 127)).astype(F32).astype(BF16)
        found = found + dot_nt(left, right)
    back = (found[:TILES] * 128.0 + found[TILES:]).astype(I32)
    for o in range(TILES):
        back_v[o] = back[o : o + 1, :]

    for copy in loads[5:]:
        copy.wait()
    for t in range(6):
        mat = ct_v[t].astype(F32)
        odd = (me // (1 << t)) % 2
        cs_v[t] = jnp.where(odd == 1, jnp.transpose(mat), mat).astype(BF16)

    def other(index):
        return index + 1 - 2 * (index % 2)

    far_half = other(group // 4)
    path = split(dot(e0_v[pos], e1_v[pos // 2]))
    f1_v[0], f1_v[1] = path
    path = times_exact(path, e2_v[pos // 4])
    links = [exact_times_turned(cs_v[3], path)]
    path = times_exact(path, e3_v[group])
    links.append(exact_times_turned(cs_v[4], path))
    path = times_exact(path, e4_v[group // 2])
    last = exact_times_turned(cs_v[5], path)
    for n in range(2):
        links.append(exact_times(e4_v[2 * far_half + n], last))
    for n in range(4):
        whi_v[R * n : R * (n + 1), :] = links[n][0]
        wlo_v[R * n : R * (n + 1), :] = links[n][1]
    loads[4].wait()
    for i in range(L_DEV):
        at = slice(LEAF * i, LEAF * (i + 1))
        hi, lo = split(dot(tl_v[i], tl_v[4 + i // 2]))
        both = fold_lanes(dot(bhi_v[at, :], jnp.concatenate([hi, lo], axis=1)))
        hi, lo = split(both + dot(blo_v[at, :], hi))
        uhi_v[at, :] = hi
        ulo_v[at, :] = lo


    take_quads(a_s, a_r, 1, slot_v, x_v)
    for o in range(TILES):
        x2_v[:, 128 * o : 128 * (o + 1)] = pair(x_v[o])

    def up(children, transfers):
        lhs = pair(jnp.concatenate(children, axis=1))
        return fold(dot(lhs, transfers.reshape(2 * R, R)))

    x2 = x2_v[...]
    q0_v[pos] = fold(dot(x2, uhi_v[...])) + dot(x2[:PRB], ulo_v[...])

    @pl.loop(1, 8)
    def _(k):
        peer = group * 8 + (pos + k) % 8
        remote(q0_v.at[pos], q0_v.at[pos], 3, peer).start()

    def near(i):
        x2 = x2_v[:, LEAF * i : LEAF * (i + 1)]
        at = slice(LEAF * i, LEAF * (i + 1))
        hi, lo = split(within[i])
        both = jnp.concatenate([hi, lo], axis=0)
        inner = fold(dot(x2, dhi_v[at, :])) + dot(x2[:PRB], dlo_v[at, :])
        inner = inner + fold(dot_nt(both, bhi_v[at, :])) + dot_nt(hi, blo_v[at, :])
        for b in range(4):
            y_v[4 * i + b] = OUTPUT_SCALE * inner[:, 128 * b : 128 * (b + 1)] + NOISE_VAR * x_v[4 * i + b]

    dense(0)

    def coupled(q, matrix):
        return fold(dot(pair(q), matrix))

    def down(g, matrix):
        return fold(dot_nt(pair(g), matrix))

    leaves = []
    for i in range(L_DEV):
        x2 = x2_v[:, LEAF * i : LEAF * (i + 1)]
        at = slice(LEAF * i, LEAF * (i + 1))
        leaves.append(fold(dot(x2, bhi_v[at, :])) + dot(x2[:PRB], blo_v[at, :]))
    mids = [up(leaves[2 * n : 2 * n + 2], tl_v[2 * n : 2 * n + 2]) for n in range(2)]
    within_mids = [coupled(mids[1], cl_v[2]), down(mids[0], cl_v[2])]
    within = []
    for n in range(2):
        within.append(coupled(leaves[2 * n + 1], cl_v[n]) + down(within_mids[n], tl_v[2 * n]))
        within.append(down(leaves[2 * n], cl_v[n]) + down(within_mids[n], tl_v[2 * n + 1]))

    remote(q0_v.at[pl.ds(0, 7)], q0_v.at[pl.ds(0, 7)], 3, me).wait()
    for n in range(4):
        q1_v[n] = up([q0_v[2 * n], q0_v[2 * n + 1]], e0_v[2 * n : 2 * n + 2])
    for n in range(2):
        q2_v[n] = up([q1_v[2 * n], q1_v[2 * n + 1]], e1_v[2 * n : 2 * n + 2])
    q3_v[group] = up([q2_v[0], q2_v[1]], e2_v[...])

    @pl.loop(1, 8)
    def _(k):
        peer = ((group + k) % 8) * 8 + pos
        remote(q3_v.at[group], q3_v.at[group], 4, peer).start()

    part = coupled(q0_v[other(pos)], cs_v[0]) + down(coupled(q1_v[other(pos // 2)], cs_v[1]), e0_v[pos])
    hi, lo = split(coupled(q2_v[other(pos // 4)], cs_v[2]))
    both = jnp.concatenate([hi, lo], axis=0)
    part = part + fold(dot_nt(both, f1_v[0])) + dot_nt(hi, f1_v[1])
    dense(1)
    dense(2)
    near(0)
    near(1)
    near(2)
    dense(3)
    near(3)
    remote(q3_v.at[pl.ds(0, 7)], q3_v.at[pl.ds(0, 7)], 4, me).wait()
    for n in range(4):
        q4_v[n] = up([q3_v[2 * n], q3_v[2 * n + 1]], e3_v[2 * n : 2 * n + 2])
    tops = [q3_v[other(group)], q4_v[other(group // 2)], q4_v[2 * far_half], q4_v[2 * far_half + 1]]
    hi, lo = split(jnp.concatenate(tops, axis=1))
    g = part + fold(dot(jnp.concatenate([hi, lo], axis=0), whi_v[...])) + dot(hi, wlo_v[...])
    hi, lo = split(g)
    far = fold(dot_nt(jnp.concatenate([hi, lo], axis=0), uhi_v[...])) + dot_nt(hi, ulo_v[...])
    for j in range(TILES):
        y_v[j] = y_v[j] + OUTPUT_SCALE * far[:, 128 * j : 128 * (j + 1)]

    def give(ks):
        tiles = [gather_tile(lambda s: y_v[s], inv_v[quad(k)]) for k in ks]
        send_tiles(tiles, ks, b_s, b_r, 2)

    @pl.loop(0, TILES // SB - 1)
    def _(i):
        give([TILES - 1 - SB * i - u for u in range(SB)])

    give(list(range(SB)))
    take_quads(b_s, b_r, 2, back_v, y_v)
    for j in range(TILES):
        out_v[:, 128 * j : 128 * (j + 1)] = y_v[j]
    sent_all(idx_s, idx_r, 0)
    sent_all(a_s, a_r, 1)
    sent_all(b_s, b_r, 2)


def body(probes, perm, points, anchors, trans_low, couple_low, trans_top, couple_top):
    vmem = pltpu.VMEM
    dma = pltpu.SemaphoreType.DMA
    return pl.pallas_call(
        kernel,
        out_shape=pltpu.VMEM((PRB, PTS), F32),
        in_specs=[pl.BlockSpec(memory_space=pl.ANY)] * 8,
        out_specs=pl.BlockSpec(memory_space=pltpu.VMEM),
        scratch_shapes=[
            vmem((TILES, 128), I32),
            vmem((8, PTS), F32),
            vmem((3, L_DEV * R), F32),
            vmem((PRB, PTS), F32),
            vmem((6, R, R), BF16),
            vmem((3, R, R), BF16),
            vmem((8, R, R), BF16),
            vmem((4, R, R), BF16),
            vmem((2, R, R), BF16),
            vmem((8, R, R), BF16),
            vmem((4, R, R), BF16),
            vmem((6, R, R), BF16),
            vmem((6, R, R), BF16),
            vmem((TILES, 1, 128), I32),
            vmem((TILES, 1, 128), I32),
            vmem((TILES, 1, 128), I32),
            vmem((TILES, 1, 128), I32),
            vmem((PTS, 8), F32),
            vmem((PTS, LEAF), BF16),
            vmem((PTS, LEAF), BF16),
            vmem((PTS, R), BF16),
            vmem((PTS, R), BF16),
            vmem((PTS, R), BF16),
            vmem((PTS, R), BF16),
            vmem((2, R, R), BF16),
            vmem((4 * R, R), BF16),
            vmem((4 * R, R), BF16),
            vmem((TILES, PRB, 128), F32),
            vmem((2 * PRB, PTS), BF16),
            vmem((TILES, PRB, 128), F32),
            vmem((TILES, PRB, 128), F32),
            vmem((N, 1, 128), I32),
            vmem((N, 1, 128), I32),
            vmem((N, 4, 128), F32),
            vmem((N, 4, 128), F32),
            vmem((N, 4, 128), F32),
            vmem((N, 4, 128), F32),
            vmem((8, PRB, R), F32),
            vmem((4, PRB, R), F32),
            vmem((2, PRB, R), F32),
            vmem((8, PRB, R), F32),
            vmem((4, PRB, R), F32),
            dma((17,)),
            dma((5,)),
            dma((5,)),
            dma((3, TILES)),
        ],
        compiler_params=pltpu.CompilerParams(
            collective_id=0, has_side_effects=True, vmem_limit_bytes=56 * 1024 * 1024
        ),
        name="hss_product",
    )(perm.reshape(TILES, 128), points, anchors, probes, trans_low, couple_low, trans_top, couple_top)


def solution(mesh):
    placed = (
        P("probe", "leaf"),
        P("leaf"),
        P(None, "leaf"),
        P(None, "leaf"),
        P("leaf", None, None, None),
        P("leaf", None, None, None),
        P(),
        P(),
    )
    return jax.shard_map(
        body, mesh=mesh, in_specs=placed, out_specs=P("probe", "leaf"), check_vma=False
    )
```

```python
import functools

import jax
import jax.numpy as jnp
from jax import lax
from jax.experimental import pallas as pl
from jax.experimental.pallas import tpu as pltpu
from jax.sharding import PartitionSpec as P

LEAF = 512
R = 128
PRB = 16
L_DEV = 4
PTS = 2048
N = 64
BLK = PTS // N
TILES = PTS // 128
SHARPNESS = 2.0
LOG2_E = 1.4426950408889634
OUTPUT_SCALE = 0.25
NOISE_VAR = 0.5
BATCHES = ((0, 8), (8, 16))
JB = 4
SB = 8
PB = 8
MESH = pl.DeviceIdType.MESH
F32 = jnp.float32
BF16 = jnp.bfloat16
I32 = jnp.int32


def dot(a, b):
    return jnp.dot(a, b, preferred_element_type=F32)


def dot_nt(a, b):
    return lax.dot_general(a, b, (((1,), (1,)), ((), ())), preferred_element_type=F32)


def split(v):
    hi = v.astype(BF16)
    lo = (v - hi.astype(F32)).astype(BF16)
    return hi, lo


def pair(v):
    hi, lo = split(v)
    return jnp.concatenate([hi, lo], axis=0)


def fold(r):
    return r[:PRB] + r[PRB:]


def fold_lanes(r):
    return r[:, :R] + r[:, R:]


def times_exact(pieces, matrix):
    r = dot(jnp.concatenate(pieces, axis=0), matrix)
    return split(r[:R] + r[R:])


def exact_times(matrix, pieces):
    return split(fold_lanes(dot(matrix, jnp.concatenate(pieces, axis=1))))


def exact_times_turned(matrix, pieces):
    return split(fold_lanes(dot_nt(matrix, jnp.concatenate(pieces, axis=0))))


def iota(shape, dim):
    return lax.broadcasted_iota(I32, shape, dim)


def swap_blocks(tile):
    lane = iota((8, 128), 1)
    row = iota((8, 128), 0)
    v0, v1 = tile[:8], tile[8:]
    low = lane < 64
    a0 = jnp.where(low, v0, pltpu.roll(v1, 64, 1))
    a1 = jnp.where(low, pltpu.roll(v0, 64, 1), v1)
    lane_bit = (lane >> 5) & 1
    same = (row >> 2) == lane_bit
    outs = []
    for a in (a0, a1):
        y = pltpu.roll(a, 4, 0)
        moved = jnp.where(lane_bit == 1, pltpu.roll(y, 32, 1), pltpu.roll(y, 96, 1))
        outs.append(jnp.where(same, a, moved))
    return outs


def gather_tile(source, index_row):
    index = jnp.broadcast_to(index_row, (8, 128))
    lane = index & 127
    tile = index >> 7
    out0 = jnp.zeros((8, 128), F32)
    out1 = jnp.zeros((8, 128), F32)
    for s in range(TILES):
        v = source(s)
        here = tile == s
        g0 = jnp.take_along_axis(v[:8], lane, axis=1, mode="promise_in_bounds")
        g1 = jnp.take_along_axis(v[8:], lane, axis=1, mode="promise_in_bounds")
        out0 = jnp.where(here, g0, out0)
        out1 = jnp.where(here, g1, out1)
    return jnp.concatenate([out0, out1], axis=0)


def near_order(v):
    return v + (v // 2) * (1 - 2 * (v % 2))


def by_lane_block(rows):
    block = iota((1, 128), 1) >> 5
    out = rows[3]
    for b in (2, 1, 0):
        out = jnp.where(block == b, rows[b], out)
    return out


def kernel(
    perm_h, points_h, anchors_h, probes_h, tl_h, cl_h, tt_h, ct_h,
    out_v,
    perm_v, points_v, anchors_v, probes_v, tl_v, cl_v,
    e0_v, e1_v, e2_v, e3_v, e4_v, ct_v, cs_v,
    slot_v, inv_v, asked_v, back_v,
    ptst_v, dhi_v, dlo_v, bhi_v, blo_v, uhi_v, ulo_v, f1_v, whi_v, wlo_v,
    x_v, x2_v, xs_v, y_v,
    idx_s, idx_r, a_s, a_r, b_s, b_r,
    q0_v, q1_v, q2_v, q3_v, q4_v,
    load_sem, send_sem, recv_sem, quad_sem,
):
    me = lax.axis_index("leaf")
    group = me // 8
    pos = me % 8

    def quad(k):
        along_z = ((me // 4) % 4 + near_order(k // 4)) % 4
        along_x = (me // 16 + near_order(k % 4)) % 4
        return along_x * 4 + along_z

    loads = [
        pltpu.make_async_copy(perm_h, perm_v, load_sem.at[0]),
        pltpu.make_async_copy(points_h, points_v.at[pl.ds(0, 3)], load_sem.at[1]),
        pltpu.make_async_copy(anchors_h, anchors_v, load_sem.at[2]),
        pltpu.make_async_copy(probes_h, probes_v, load_sem.at[3]),
        pltpu.make_async_copy(tl_h.at[0], tl_v, load_sem.at[4]),
        pltpu.make_async_copy(cl_h.at[0], cl_v, load_sem.at[5]),
        pltpu.make_async_copy(tt_h.at[pl.ds(group * 8, 8)], e0_v, load_sem.at[6]),
        pltpu.make_async_copy(tt_h.at[pl.ds(64 + group * 4, 4)], e1_v, load_sem.at[7]),
        pltpu.make_async_copy(tt_h.at[pl.ds(96 + group * 2, 2)], e2_v, load_sem.at[8]),
        pltpu.make_async_copy(tt_h.at[pl.ds(112, 8)], e3_v, load_sem.at[9]),
        pltpu.make_async_copy(tt_h.at[pl.ds(120, 4)], e4_v, load_sem.at[10]),
    ]
    for t, start in enumerate((0, 32, 48, 56, 60, 62)):
        loads.append(
            pltpu.make_async_copy(
                ct_h.at[pl.ds(start + me // (2 << t), 1)], ct_v.at[pl.ds(t, 1)], load_sem.at[11 + t]
            )
        )
    for copy in loads:
        copy.start()

    barrier = pltpu.get_barrier_semaphore()

    def greet(peer):
        pl.semaphore_signal(barrier, inc=1, device_id={"leaf": peer}, device_id_type=MESH)

    @pl.loop(0, TILES - 1)
    def _(i):
        for h in range(4):
            greet(4 * quad(TILES - 1 - i) + h)

    for h in range(4):
        peer = 4 * quad(0) + h
        pl.when(peer != me)(functools.partial(greet, peer))


    def remote(src, dst, which, peer, landed=None):
        return pltpu.make_async_remote_copy(
            src_ref=src, dst_ref=dst, send_sem=send_sem.at[which],
            recv_sem=recv_sem.at[which] if landed is None else landed,
            device_id={"leaf": peer}, device_id_type=MESH,
        )

    def send_quad(k, s_ref, r_ref, which):
        o = quad(k)
        for h in range(4):
            peer = 4 * o + h

            def start():
                remote(s_ref.at[peer], r_ref.at[me], which, peer, quad_sem.at[which, me // 4]).start()

            if isinstance(k, int) and k == 0:
                pl.when(peer != me)(start)
            else:
                start()

    def await_quad(k, s_ref, r_ref, which):
        count = 3 if isinstance(k, int) and k == 0 else 4
        o = quad(k)
        at = pl.ds(0, count)
        remote(s_ref.at[at], r_ref.at[at], which, me, quad_sem.at[which, o]).wait_recv()
        return o

    def sent_all(s_ref, r_ref, which):
        at = pl.ds(0, N - 1)
        remote(s_ref.at[at], r_ref.at[at], which, me).wait_send()

    loads[0].wait()
    row64 = iota((N, 128), 0)
    lane1 = iota((1, 128), 1)
    ones = []
    for b in range(TILES):
        home = perm_v[b : b + 1, :] >> 11
        ones.append((row64 == home).astype(F32))
    before = (iota((128, 128), 0) < iota((128, 128), 1)).astype(BF16)
    counter = jnp.concatenate([before, jnp.ones((128, 128), BF16)], axis=1)
    counts = dot(jnp.concatenate(ones, axis=0).astype(BF16), counter)
    base = jnp.zeros((N, 128), F32)
    found = jnp.zeros((4 * N, 128), F32)
    row128 = iota((128, 128), 0) & (BLK - 1)
    for b in range(TILES):
        entry = perm_v[b : b + 1, :]
        one = ones[b]
        rank = jnp.sum(one * (counts[N * b : N * (b + 1), :128] + base), axis=0, keepdims=True)
        base = base + counts[N * b : N * (b + 1), 128:]
        rank = rank.astype(I32)
        slot_v[b] = (entry >> 11) * BLK + rank
        offset = entry & (PTS - 1)
        left = jnp.concatenate(
            [
                one * (offset >> 8).astype(F32),
                one * (offset & 255).astype(F32),
                one * float(b),
                one * lane1.astype(F32),
            ],
            axis=0,
        ).astype(BF16)
        right = (row128 == rank).astype(F32).astype(BF16)
        found = found + dot_nt(left, right)
    wanted = (found[:N] * 256.0 + found[N : 2 * N]).astype(I32)
    places = (found[2 * N : 3 * N] * 128.0 + found[3 * N :]).astype(I32)
    for h in range(N):
        idx_s[h] = wanted[h : h + 1, :]
    for o in range(TILES):
        inv_v[o] = by_lane_block([places[4 * o + b : 4 * o + b + 1, :] for b in range(4)])

    pl.semaphore_wait(barrier, N - 1)

    @pl.loop(0, TILES - 1)
    def _(i):
        send_quad(TILES - 1 - i, idx_s, idx_r, 0)

    send_quad(0, idx_s, idx_r, 0)
    idx_r[me] = idx_s[me]

    loads[1].wait()
    loads[2].wait()
    for b in range(TILES):
        ptst_v[128 * b : 128 * (b + 1), :] = jnp.transpose(points_v[:, 128 * b : 128 * (b + 1)])

    rows = 256

    @pl.loop(0, PTS // rows)
    def _(i):
        at = pl.ds(pl.multiple_of(i * rows, rows), rows)
        leaf = i // (LEAF // rows)
        total = None
        for c in range(3):
            left = ptst_v[at, c : c + 1]
            right = anchors_v[c : c + 1, pl.ds(pl.multiple_of(leaf * R, R), R)]
            differ = left - right
            total = differ * differ if total is None else total + differ * differ
        hi, lo = split(jnp.exp2((-SHARPNESS * LOG2_E) * total))
        bhi_v[at, :] = hi
        blo_v[at, :] = lo

    drows = 128

    half = LEAF // 2

    def dense(leaf):
        for start, skip in ((0, 0), (half, half)):

            @pl.loop(0, half // drows)
            def _(i):
                at = pl.ds(pl.multiple_of(leaf * LEAF + start + i * drows, drows), drows)
                total = None
                for c in range(3):
                    left = ptst_v[at, c : c + 1]
                    right = points_v[c : c + 1, leaf * LEAF + skip : (leaf + 1) * LEAF]
                    differ = left - right
                    total = differ * differ if total is None else total + differ * differ
                hi, lo = split(jnp.exp2((-SHARPNESS * LOG2_E) * total))
                dhi_v[at, skip:] = hi
                dlo_v[at, skip:] = lo

    loads[3].wait()

    def send_tiles(tiles, ks, s_ref, r_ref, which):
        for tile, k in zip(tiles, ks):
            o = quad(k)
            halves = swap_blocks(tile)
            for h in range(4):
                s_ref[4 * o + h] = halves[h // 2][4 * (h % 2) : 4 * (h % 2) + 4]
        for k in ks:
            send_quad(k, s_ref, r_ref, which)

    def take_quads(s_ref, r_ref, which, slots, out):
        r_ref[me] = s_ref[me]
        for first, last in BATCHES:
            ks = range(first, last)
            homes = [await_quad(k, s_ref, r_ref, which) for k in ks]
            for k, o in zip(ks, homes):
                both = swap_blocks(jnp.concatenate([r_ref[4 * o + h] for h in range(4)], axis=0))
                xs_v[k] = jnp.concatenate(both, axis=0)

            @pl.loop(0, TILES // JB)
            def _(i):
                for u in range(JB):
                    j = i * JB + u
                    index = jnp.broadcast_to(slots[j], (8, 128))
                    lane = index & 127
                    tile = index >> 7
                    got = [out[j, 8 * v : 8 * v + 8] if first else jnp.zeros((8, 128), F32) for v in range(2)]
                    for k, o in zip(ks, homes):
                        here = tile == o
                        for v in range(2):
                            part = jnp.take_along_axis(
                                xs_v[k, 8 * v : 8 * v + 8], lane, axis=1, mode="promise_in_bounds"
                            )
                            got[v] = jnp.where(here, part, got[v])
                    for v in range(2):
                        out[j, 8 * v : 8 * v + 8] = got[v]

    def pick(ks):
        tiles = []
        for k in ks:
            o = await_quad(k, idx_s, idx_r, 0)
            asked = by_lane_block([idx_r[4 * o + b] for b in range(4)])
            asked_v[o] = asked
            tiles.append(gather_tile(lambda s: probes_v[:, 128 * s : 128 * (s + 1)], asked))
        send_tiles(tiles, ks, a_s, a_r, 1)

    pick(list(range(PB)))

    @pl.loop(1, TILES // PB)
    def _(i):
        pick([PB * i + u for u in range(PB)])


    found = jnp.zeros((2 * TILES, 128), F32)
    row16 = iota((TILES, 128), 0)
    row128 = iota((128, 128), 0)
    for o in range(TILES):
        asked = asked_v[o]
        one = (row16 == (asked >> 7)).astype(F32)
        left = jnp.concatenate([one * float(o), one * lane1.astype(F32)], axis=0).astype(BF16)
        right = (row128 == (asked & 127)).astype(F32).astype(BF16)
        found = found + dot_nt(left, right)
    back = (found[:TILES] * 128.0 + found[TILES:]).astype(I32)
    for o in range(TILES):
        back_v[o] = back[o : o + 1, :]

    for copy in loads[5:]:
        copy.wait()
    for t in range(6):
        mat = ct_v[t].astype(F32)
        odd = (me // (1 << t)) % 2
        cs_v[t] = jnp.where(odd == 1, jnp.transpose(mat), mat).astype(BF16)

    def other(index):
        return index + 1 - 2 * (index % 2)

    far_half = other(group // 4)
    path = split(dot(e0_v[pos], e1_v[pos // 2]))
    f1_v[0], f1_v[1] = path
    path = times_exact(path, e2_v[pos // 4])
    links = [exact_times_turned(cs_v[3], path)]
    path = times_exact(path, e3_v[group])
    links.append(exact_times_turned(cs_v[4], path))
    path = times_exact(path, e4_v[group // 2])
    last = exact_times_turned(cs_v[5], path)
    for n in range(2):
        links.append(exact_times(e4_v[2 * far_half + n], last))
    for n in range(4):
        whi_v[R * n : R * (n + 1), :] = links[n][0]
        wlo_v[R * n : R * (n + 1), :] = links[n][1]
    loads[4].wait()
    for i in range(L_DEV):
        at = slice(LEAF * i, LEAF * (i + 1))
        hi, lo = split(dot(tl_v[i], tl_v[4 + i // 2]))
        both = fold_lanes(dot(bhi_v[at, :], jnp.concatenate([hi, lo], axis=1)))
        hi, lo = split(both + dot(blo_v[at, :], hi))
        uhi_v[at, :] = hi
        ulo_v[at, :] = lo


    take_quads(a_s, a_r, 1, slot_v, x_v)
    for o in range(TILES):
        x2_v[:, 128 * o : 128 * (o + 1)] = pair(x_v[o])

    def up(children, transfers):
        lhs = pair(jnp.concatenate(children, axis=1))
        return fold(dot(lhs, transfers.reshape(2 * R, R)))

    x2 = x2_v[...]
    q0_v[pos] = fold(dot(x2, uhi_v[...])) + dot(x2[:PRB], ulo_v[...])

    @pl.loop(1, 8)
    def _(k):
        peer = group * 8 + (pos + k) % 8
        remote(q0_v.at[pos], q0_v.at[pos], 3, peer).start()

    def near(i):
        x2 = x2_v[:, LEAF * i : LEAF * (i + 1)]
        at = slice(LEAF * i, LEAF * (i + 1))
        hi, lo = split(within[i])
        both = jnp.concatenate([hi, lo], axis=0)
        upper = slice(LEAF * i, LEAF * i + half)
        first = fold(dot(x2[:, :half], dhi_v[upper, :half])) + dot(x2[:PRB, :half], dlo_v[upper, :half])
        first = first + fold(dot_nt(x2[:, half:], dhi_v[upper, half:])) + dot_nt(x2[:PRB, half:], dlo_v[upper, half:])
        second = fold(dot(x2, dhi_v[at, half:])) + dot(x2[:PRB], dlo_v[at, half:])
        inner = jnp.concatenate([first, second], axis=1)
        inner = inner + fold(dot_nt(both, bhi_v[at, :])) + dot_nt(hi, blo_v[at, :])
        for b in range(4):
            y_v[4 * i + b] = OUTPUT_SCALE * inner[:, 128 * b : 128 * (b + 1)] + NOISE_VAR * x_v[4 * i + b]

    dense(0)

    def coupled(q, matrix):
        return fold(dot(pair(q), matrix))

    def down(g, matrix):
        return fold(dot_nt(pair(g), matrix))

    leaves = []
    for i in range(L_DEV):
        x2 = x2_v[:, LEAF * i : LEAF * (i + 1)]
        at = slice(LEAF * i, LEAF * (i + 1))
        leaves.append(fold(dot(x2, bhi_v[at, :])) + dot(x2[:PRB], blo_v[at, :]))
    mids = [up(leaves[2 * n : 2 * n + 2], tl_v[2 * n : 2 * n + 2]) for n in range(2)]
    within_mids = [coupled(mids[1], cl_v[2]), down(mids[0], cl_v[2])]
    within = []
    for n in range(2):
        within.append(coupled(leaves[2 * n + 1], cl_v[n]) + down(within_mids[n], tl_v[2 * n]))
        within.append(down(leaves[2 * n], cl_v[n]) + down(within_mids[n], tl_v[2 * n + 1]))

    remote(q0_v.at[pl.ds(0, 7)], q0_v.at[pl.ds(0, 7)], 3, me).wait()
    for n in range(4):
        q1_v[n] = up([q0_v[2 * n], q0_v[2 * n + 1]], e0_v[2 * n : 2 * n + 2])
    for n in range(2):
        q2_v[n] = up([q1_v[2 * n], q1_v[2 * n + 1]], e1_v[2 * n : 2 * n + 2])
    q3_v[group] = up([q2_v[0], q2_v[1]], e2_v[...])

    @pl.loop(1, 8)
    def _(k):
        peer = ((group + k) % 8) * 8 + pos
        remote(q3_v.at[group], q3_v.at[group], 4, peer).start()

    part = coupled(q0_v[other(pos)], cs_v[0]) + down(coupled(q1_v[other(pos // 2)], cs_v[1]), e0_v[pos])
    hi, lo = split(coupled(q2_v[other(pos // 4)], cs_v[2]))
    both = jnp.concatenate([hi, lo], axis=0)
    part = part + fold(dot_nt(both, f1_v[0])) + dot_nt(hi, f1_v[1])
    dense(1)
    dense(2)
    near(0)
    near(1)
    near(2)
    dense(3)
    near(3)
    remote(q3_v.at[pl.ds(0, 7)], q3_v.at[pl.ds(0, 7)], 4, me).wait()
    for n in range(4):
        q4_v[n] = up([q3_v[2 * n], q3_v[2 * n + 1]], e3_v[2 * n : 2 * n + 2])
    tops = [q3_v[other(group)], q4_v[other(group // 2)], q4_v[2 * far_half], q4_v[2 * far_half + 1]]
    hi, lo = split(jnp.concatenate(tops, axis=1))
    g = part + fold(dot(jnp.concatenate([hi, lo], axis=0), whi_v[...])) + dot(hi, wlo_v[...])
    hi, lo = split(g)
    far = fold(dot_nt(jnp.concatenate([hi, lo], axis=0), uhi_v[...])) + dot_nt(hi, ulo_v[...])
    for j in range(TILES):
        y_v[j] = y_v[j] + OUTPUT_SCALE * far[:, 128 * j : 128 * (j + 1)]

    def give(ks):
        tiles = [gather_tile(lambda s: y_v[s], inv_v[quad(k)]) for k in ks]
        send_tiles(tiles, ks, b_s, b_r, 2)

    @pl.loop(0, TILES // SB - 1)
    def _(i):
        give([TILES - 1 - SB * i - u for u in range(SB)])

    give(list(range(SB)))
    take_quads(b_s, b_r, 2, back_v, y_v)
    for j in range(TILES):
        out_v[:, 128 * j : 128 * (j + 1)] = y_v[j]
    sent_all(idx_s, idx_r, 0)
    sent_all(a_s, a_r, 1)
    sent_all(b_s, b_r, 2)


def body(probes, perm, points, anchors, trans_low, couple_low, trans_top, couple_top):
    vmem = pltpu.VMEM
    dma = pltpu.SemaphoreType.DMA
    return pl.pallas_call(
        kernel,
        out_shape=pltpu.VMEM((PRB, PTS), F32),
        in_specs=[pl.BlockSpec(memory_space=pl.ANY)] * 8,
        out_specs=pl.BlockSpec(memory_space=pltpu.VMEM),
        scratch_shapes=[
            vmem((TILES, 128), I32),
            vmem((8, PTS), F32),
            vmem((3, L_DEV * R), F32),
            vmem((PRB, PTS), F32),
            vmem((6, R, R), BF16),
            vmem((3, R, R), BF16),
            vmem((8, R, R), BF16),
            vmem((4, R, R), BF16),
            vmem((2, R, R), BF16),
            vmem((8, R, R), BF16),
            vmem((4, R, R), BF16),
            vmem((6, R, R), BF16),
            vmem((6, R, R), BF16),
            vmem((TILES, 1, 128), I32),
            vmem((TILES, 1, 128), I32),
            vmem((TILES, 1, 128), I32),
            vmem((TILES, 1, 128), I32),
            vmem((PTS, 8), F32),
            vmem((PTS, LEAF), BF16),
            vmem((PTS, LEAF), BF16),
            vmem((PTS, R), BF16),
            vmem((PTS, R), BF16),
            vmem((PTS, R), BF16),
            vmem((PTS, R), BF16),
            vmem((2, R, R), BF16),
            vmem((4 * R, R), BF16),
            vmem((4 * R, R), BF16),
            vmem((TILES, PRB, 128), F32),
            vmem((2 * PRB, PTS), BF16),
            vmem((TILES, PRB, 128), F32),
            vmem((TILES, PRB, 128), F32),
            vmem((N, 1, 128), I32),
            vmem((N, 1, 128), I32),
            vmem((N, 4, 128), F32),
            vmem((N, 4, 128), F32),
            vmem((N, 4, 128), F32),
            vmem((N, 4, 128), F32),
            vmem((8, PRB, R), F32),
            vmem((4, PRB, R), F32),
            vmem((2, PRB, R), F32),
            vmem((8, PRB, R), F32),
            vmem((4, PRB, R), F32),
            dma((17,)),
            dma((5,)),
            dma((5,)),
            dma((3, TILES)),
        ],
        compiler_params=pltpu.CompilerParams(
            collective_id=0, has_side_effects=True, vmem_limit_bytes=56 * 1024 * 1024
        ),
        name="hss_product",
    )(perm.reshape(TILES, 128), points, anchors, probes, trans_low, couple_low, trans_top, couple_top)


def solution(mesh):
    placed = (
        P("probe", "leaf"),
        P("leaf"),
        P(None, "leaf"),
        P(None, "leaf"),
        P("leaf", None, None, None),
        P("leaf", None, None, None),
        P(),
        P(),
    )
    return jax.shard_map(
        body, mesh=mesh, in_specs=placed, out_specs=P("probe", "leaf"), check_vma=False
    )
```
